32 devices in a mesh: row: 16 (over z, y, x), col: 2 (over core).
Axes of the slice: x: 2, y: 2, z: 4, core: 2. Of those that a mesh axis runs over, the one named last changes fastest.
Arguments:
- slab: bfloat16 [65536, 2048], P('row', 'col'), may hold values from -6 to 6
- gauss: bfloat16 [2048, 1024], P('col'), may hold values from -0.125 to 0.125
- pivots: int32 [1024], replicated, may hold values from 0 to 65535, as said below
- block_inverses: float32 [8, 128, 128], replicated, may hold values from -2 to 2
Outputs:
- factor_rows: float32 [65536, 1024], P(('row', 'col'))
- pivot_block: float32 [1024, 1024], P(('row', 'col'))
The draws below stay inside these ranges and needn't reach their ends.
Inputs may be any that keep to these rules, and one draw needn't show every extreme that they name: `pivots`: distinct row numbers; each aligned block of 2048 rows holds at most 128 of them, and some block holds exactly 128.
All inputs are finite; a program needn't handle non-finite values.
Results may differ from the reference program's by a relative error of at most 0.0003.
Values may be sent and summed in bfloat16 or wider, within the bound.
No kernel may reach another device: no remote copies, remote signals or barrier semaphores. Data moves between devices by JAX's collectives and lax.ppermute only.
A program may use at most 128 MiB of HBM per device.

```python
import jax
import jax.numpy as jnp
import numpy as np
from jax import lax

K = 1024
SLAB = 2048
BLK = 128
NROWS = 65536
SHARD_ROWS = 2048
PIV_MOST = 128


def draw_pivots(key, part):
    blocks = NROWS // SHARD_ROWS
    remain = K - PIV_MOST
    base = remain // (blocks - 1)
    extra = remain - base * (blocks - 1)
    pattern = np.array([PIV_MOST] + [base + 1] * extra + [base] * (blocks - 1 - extra), dtype=np.int32)
    key_order = jax.random.fold_in(key, 11)
    key_rank = jax.random.fold_in(key, 12)
    key_shuffle = jax.random.fold_in(key, 13)
    order = jax.random.permutation(key_order, blocks)
    counts = jnp.asarray(pattern)[order]
    scores = jax.random.randint(key_rank, (blocks, SHARD_ROWS), 0, 1 << 20) * SHARD_ROWS + jnp.arange(SHARD_ROWS, dtype=jnp.int32)[None, :]
    ranks = jnp.argsort(jnp.argsort(scores, axis=1, stable=True), axis=1, stable=True)
    chosen = (ranks < counts[:, None]).reshape(-1)
    picked = jnp.nonzero(chosen, size=K, fill_value=0)[0].astype(jnp.int32)
    shuffle = jax.random.permutation(key_shuffle, K)
    return picked[shuffle].astype(jnp.int32)


def draw_block_inverses(key, part):
    count = K // BLK
    key_diag = jax.random.fold_in(key, 21)
    key_off = jax.random.fold_in(key, 22)
    diag = jax.random.uniform(key_diag, (count, BLK), jnp.float32, 0.6, 1.4)
    off = jax.random.normal(key_off, (count, BLK, BLK), jnp.float32) * (0.6 / BLK ** 0.5)
    rows = jnp.arange(BLK)[:, None]
    cols = jnp.arange(BLK)[None, :]
    upper = jnp.where(cols > rows, off, 0.0)
    eye = jnp.where(cols == rows, 1.0, 0.0)
    return (upper + diag[:, :, None] * eye[None, :, :]).astype(jnp.float32)


def level_of(key, dims, pieces, least, high):
    factor_of = 1.0
    for dim, blocks in pieces:
        heights = jax.random.uniform(jax.random.fold_in(jax.random.fold_in(key, 6), dim), (blocks,), jnp.float32, least / len(pieces), high / len(pieces))
        factor_of = factor_of * jnp.repeat(jnp.exp(heights), dims[dim] // blocks).reshape((-1,) + (1,) * (len(dims) - 1 - dim))
    return factor_of


def noise(key, dims, deviation, reach, cuts=(), kind=jnp.bfloat16):
    values = jax.random.normal(key, dims, jnp.float32) * deviation
    if len(cuts) > 0:
        values = level_of(key, dims, cuts, -0.22, 0.18) * values
    return jnp.clip(values, min=-reach, max=reach).astype(kind)


def setup_inputs(seed: int = 0) -> dict:
    arg_keys = jax.random.split(jax.random.key(seed), 5)
    return {
        "slab": noise(arg_keys[0], (NROWS, SLAB), 1.0, 6.0, ((0, 16), (1, 2))),
        "gauss": noise(arg_keys[1], (SLAB, K), SLAB ** -0.5, 0.125, ((0, 2),)),
        "pivots": draw_pivots(jax.random.fold_in(arg_keys[4], 71), 0),
        "block_inverses": draw_block_inverses(jax.random.fold_in(arg_keys[4], 71), 0),
    }


def reference(slab, gauss, pivots, block_inverses):
    sketch = jnp.dot(slab, gauss, preferred_element_type=jnp.float32)
    pivot_block = jnp.take(sketch, pivots, axis=0)
    factor = 1.0 / (K ** 0.5)
    solved = []
    for block in range(K // BLK):
        acc = sketch[:, block * BLK:(block + 1) * BLK]
        if block > 0:
            earlier = jnp.concatenate(solved, axis=1)
            coupling = pivot_block[:block * BLK, block * BLK:(block + 1) * BLK]
            acc = acc - factor * jnp.dot(earlier, coupling, precision=lax.Precision.HIGHEST)
        solved.append(jnp.dot(acc, block_inverses[block], precision=lax.Precision.HIGHEST))
    return jnp.concatenate(solved, axis=1), pivot_block
```

```python
import jax
import jax.numpy as jnp
from jax import lax
from jax.experimental import pallas as pl
from jax.experimental.pallas import tpu as pltpu
from jax.sharding import PartitionSpec as P

K = 1024
BLK = 128
NBLK = K // BLK
SHARD_ROWS = 2048
PIV_MOST = 128
SUB = 16
UPPER = [(i, j) for i in range(NBLK) for j in range(i + 1, NBLK)]
F32 = jnp.float32
BF16 = jnp.bfloat16
MIB = 1 << 20


def dot(a, b, dims=((1,), (0,))):
    return lax.dot_general(a, b, (dims, ((), ())), preferred_element_type=F32)


def split(a):
    high = a.astype(BF16)
    return high, (a - high.astype(F32)).astype(BF16)


def group_slot(group, x, y, c):
    gy, gx, gc = group >> 2, (group >> 1) & 1, group & 1
    dx, dy, dc = gx ^ x, gy ^ y, gc ^ c
    return dc * 4 + (dx * 2 + dy if gc == 0 else dy * 2 + dx)


def slot_group(slot, x, y, c):
    dc, high, low = slot >> 2, (slot >> 1) & 1, slot & 1
    gc = c ^ dc
    dx = jnp.where(gc == 0, high, low)
    dy = jnp.where(gc == 0, low, high)
    return (y ^ dy) * 4 + (x ^ dx) * 2 + gc


def lower_layout(share):
    tops = K // (8 * share)
    return [-(-((z + 1) * 8 * share) // BLK) for z in range(tops)]


def pick_kernel(share, meta, piv, slab, gauss, u_keep, u_send, l_keep, l_send,
                slab_v, gauss_v, rows_v, u_scr, l_scr, sems):
    r, c = meta[0], meta[1]
    x, y = r & 1, (r >> 1) & 1
    copies = [
        pltpu.make_async_copy(
            slab.at[pl.ds(t * 1024, 1024)], slab_v.at[pl.ds(t * 1024, 1024)], sems.at[t])
        for t in range(4)
    ]
    copies.append(pltpu.make_async_copy(gauss, gauss_v, sems.at[4]))
    for copy in copies:
        copy.start()

    half = lax.broadcasted_iota(jnp.int32, (8, K), 0)
    local = piv[...] - (r * (2 * SHARD_ROWS) + half * SHARD_ROWS)
    inside = (local >= 0) & (local < SHARD_ROWS) & (half < 2)
    earlier = lax.broadcasted_iota(jnp.int32, (K, K), 0) < lax.broadcasted_iota(jnp.int32, (K, K), 1)
    rank = dot(jnp.where(inside, 1.0, 0.0).astype(BF16), jnp.where(earlier, 1.0, 0.0).astype(BF16))
    rank = jnp.where(inside, rank, -1.0)
    order = lax.broadcasted_iota(jnp.int32, (PIV_MOST, K), 0).astype(F32)
    rows = lax.broadcasted_iota(jnp.int32, (PIV_MOST, SHARD_ROWS), 1).astype(F32)
    place, picks = [], []
    for b in range(2):
        hit = rank[b:b + 1, :] == order
        place.append(jnp.where(hit, 1.0, 0.0).astype(BF16))
        row = jnp.sum(jnp.where(hit, local[b:b + 1, :].astype(F32), 0.0), axis=1, keepdims=True)
        picks.append(jnp.where(rows == row, 1.0, 0.0).astype(BF16))
    packed = []
    for b in range(2):
        copies[2 * b].wait()
        part = dot(picks[b][:, :1024], slab_v[pl.ds(b * 2048, 1024), :])
        copies[2 * b + 1].wait()
        part = part + dot(picks[b][:, 1024:], slab_v[pl.ds(b * 2048 + 1024, 1024), :])
        packed.append(part.astype(BF16))
    packed = jnp.concatenate(packed, axis=0)
    place = jnp.concatenate(place, axis=0)
    copies[4].wait()
    for t in range(4):
        spread = dot(place[:, t * 256:(t + 1) * 256], packed, ((0,), (0,))).astype(BF16)
        rows_v[pl.ds(t * 256, 256), :] = dot(spread, gauss_v[...])

    columns = lower_layout(share)
    for group in range(8):
        slot = group_slot(group, x, y, c)
        for n, (i, j) in enumerate(UPPER):
            u_scr[slot, n] = rows_v[pl.ds(i * BLK + group * SUB, SUB), pl.ds(j * BLK, BLK)]
        n = 0
        for z, count in enumerate(columns):
            for j in range(count):
                l_scr[slot, n] = rows_v[pl.ds((z * 8 + group) * share, share), pl.ds(j * BLK, BLK)]
                n += 1
    u_keep[...] = u_scr[0:4]
    u_send[...] = u_scr[4:8]
    l_keep[...] = l_scr[0:4]
    l_send[...] = l_scr[4:8]


def pick(meta, piv, slab, gauss, share):
    units = sum(lower_layout(share))
    u_shape = jax.ShapeDtypeStruct((4, len(UPPER), SUB, BLK), F32)
    l_shape = jax.ShapeDtypeStruct((4, units, share, BLK), F32)
    vmem = pl.BlockSpec(memory_space=pltpu.VMEM)
    return pl.pallas_call(
        lambda *refs: pick_kernel(share, *refs),
        out_shape=(u_shape, u_shape, l_shape, l_shape),
        in_specs=[pl.BlockSpec(memory_space=pltpu.SMEM), vmem,
                  pl.BlockSpec(memory_space=pl.ANY), pl.BlockSpec(memory_space=pl.ANY)],
        out_specs=(vmem,) * 4,
        scratch_shapes=[
            pltpu.VMEM((2 * SHARD_ROWS, K), BF16),
            pltpu.VMEM((K, K), BF16),
            pltpu.VMEM((K, K), F32),
            pltpu.VMEM((8, len(UPPER), SUB, BLK), F32),
            pltpu.VMEM((8, units, share, BLK), F32),
            pltpu.SemaphoreType.DMA((5,)),
        ],
        compiler_params=pltpu.CompilerParams(vmem_limit_bytes=44 * MIB),
        cost_estimate=pl.CostEstimate(flops=6 * 10**9, bytes_accessed=16 * MIB, transcendentals=0),
        name="pick_pivot_rows",
    )(meta, piv, slab, gauss)


def sketch_kernel(meta, mine, theirs, gauss_mine, gauss_theirs, out):
    out[...] = dot(mine[...], gauss_mine[...]) + dot(theirs[...], gauss_theirs[...])


def sketch_rows(meta, slab, theirs, gauss_mine, gauss_theirs):
    rows, depth = theirs.shape
    tile = 256
    whole = pl.BlockSpec((depth, K), lambda t, meta: (0, 0))
    return pl.pallas_call(
        sketch_kernel,
        out_shape=jax.ShapeDtypeStruct((rows, K), F32),
        grid_spec=pltpu.PrefetchScalarGridSpec(
            num_scalar_prefetch=1,
            grid=(rows // tile,),
            in_specs=[
                pl.BlockSpec((tile, depth), lambda t, meta: (meta[1] * (rows // tile) + t, 0)),
                pl.BlockSpec((tile, depth), lambda t, meta: (t, 0)),
                whole, whole,
            ],
            out_specs=pl.BlockSpec((tile, K), lambda t, meta: (t, 0)),
        ),
        compiler_params=pltpu.CompilerParams(vmem_limit_bytes=32 * MIB),
        cost_estimate=pl.CostEstimate(
            flops=4 * rows * depth * K, bytes_accessed=20 * MIB, transcendentals=0),
        name="sketch_rows",
    )(meta, slab, theirs, gauss_mine, gauss_theirs)


def product(a, b):
    return dot(a[0], b[0]) + (dot(a[1], b[0]) + dot(a[0], b[1]))


def solve_kernel(share, meta, sketch, inverses, p0, p1, p2, p3, out, own_rows,
                 coupling, c_high, c_low, d_high, d_low, f_high, f_low):
    r, c = meta[0], meta[1]
    x, y = r & 1, (r >> 1) & 1

    @pl.when(pl.program_id(0) == 0)
    def _():
        coupling[...] = jnp.zeros_like(coupling)
        slot = 0
        for piece in (p0, p1, p2, p3):
            for k in range(piece.shape[0]):
                group = slot_group(slot, x, y, c)
                for n, (i, j) in enumerate(UPPER):
                    at = pl.multiple_of(i * BLK + group * SUB, SUB)
                    coupling[pl.ds(at, SUB), pl.ds(j * BLK, BLK)] = piece[k, n]
                slot += 1
        own = pl.multiple_of((r * 2 + c) * share, share)
        own_rows[...] = coupling[pl.ds(own, share), :]
        scaled = coupling[...] * (-1.0 / K**0.5)
        c_high[...], c_low[...] = split(scaled)
        for s in range(NBLK // 2):
            first, second = inverses[2 * s], inverses[2 * s + 1]
            link = coupling[pl.ds(2 * s * BLK, BLK), pl.ds((2 * s + 1) * BLK, BLK)]
            link = link * (-1.0 / K**0.5)
            highest = dict(precision=lax.Precision.HIGHEST, preferred_element_type=F32)
            corner = jnp.dot(first, jnp.dot(link, second, **highest), **highest)
            for at, value in ((0, first), (1, corner), (3, second), (2, jnp.zeros_like(first))):
                high, low = split(value)
                spot = (s, pl.ds((at >> 1) * BLK, BLK), pl.ds((at & 1) * BLK, BLK))
                d_high[spot] = high
                d_low[spot] = low

    wide = 2 * BLK
    for s in range(NBLK // 2):
        cols = pl.ds(s * wide, wide)
        acc = sketch[:, cols]
        if s > 0:
            before = pl.ds(0, s * wide)
            acc = acc + product((f_high[:, before], f_low[:, before]),
                                (c_high[before, cols], c_low[before, cols]))
        solved = product(split(acc), (d_high[s], d_low[s]))
        out[:, cols] = solved
        if s < NBLK // 2 - 1:
            f_high[:, cols], f_low[:, cols] = split(solved)


def solve(meta, sketch, inverses, pieces, share):
    rows = sketch.shape[0]
    tile = 512
    wide = 2 * BLK

    def whole(a):
        return pl.BlockSpec(a.shape, lambda t, meta, n=a.ndim: (0,) * n)

    return pl.pallas_call(
        lambda *refs: solve_kernel(share, *refs),
        out_shape=(jax.ShapeDtypeStruct((rows, K), F32), jax.ShapeDtypeStruct((share, K), F32)),
        grid_spec=pltpu.PrefetchScalarGridSpec(
            num_scalar_prefetch=1,
            grid=(rows // tile,),
            in_specs=[pl.BlockSpec((tile, K), lambda t, meta: (t, 0)), whole(inverses)]
            + [whole(p) for p in pieces],
            out_specs=(pl.BlockSpec((tile, K), lambda t, meta: (t, 0)),
                       pl.BlockSpec((share, K), lambda t, meta: (0, 0))),
            scratch_shapes=[
                pltpu.VMEM((K, K), F32),
                pltpu.VMEM((K, K), BF16),
                pltpu.VMEM((K, K), BF16),
                pltpu.VMEM((NBLK // 2, wide, wide), BF16),
                pltpu.VMEM((NBLK // 2, wide, wide), BF16),
                pltpu.VMEM((tile, K), BF16),
                pltpu.VMEM((tile, K), BF16),
            ],
        ),
        compiler_params=pltpu.CompilerParams(vmem_limit_bytes=48 * MIB),
        cost_estimate=pl.CostEstimate(flops=8 * 10**9, bytes_accessed=20 * MIB, transcendentals=0),
        name="blocked_solve",
    )(meta, sketch, inverses, *pieces)


def on_device(slab, gauss, pivots, block_inverses):
    rows = lax.axis_size("row")
    cols = lax.axis_size("col")
    bits = rows.bit_length() - 1
    share = K // (rows * cols)
    r, c = lax.axis_index("row"), lax.axis_index("col")
    meta = jnp.stack([r, c]).astype(jnp.int32)

    def swap(value, bit_of):
        perm = [(2 * i + k, 2 * (i ^ (1 << bit_of[k])) + k) for i in range(rows) for k in range(2)]
        return lax.ppermute(value, ("row", "col"), perm)

    def swap_cores(value):
        return lax.ppermute(value, "col", [(0, 1), (1, 0)])

    near, far = (0, 1), (1, 0)
    tops = bits - 2
    climb = [(2 + s, 2 + (s + 1) % tops) for s in range(tops)]

    u_keep, u_send, l_keep, l_send = pick(meta, pivots.reshape(1, K), slab, gauss, share)

    u_got = swap_cores(u_send)
    send = u_keep[2:4] + u_got[2:4]
    got = swap(send, near)
    send = (u_keep[1:2] + u_got[1:2]) + got[1:2]
    kept = (u_keep[0:1] + u_got[0:1]) + got[0:1]
    total = kept + swap(send, far)
    for bit_of in climb:
        total = total + swap(total, bit_of)
    piece1 = swap(total, far)
    pair = jnp.concatenate([total, piece1], axis=0)
    piece2 = swap(pair, near)
    piece3 = swap_cores(jnp.concatenate([pair, piece2], axis=0))

    own = slab.shape[0] // cols
    slab_theirs = swap_cores(lax.dynamic_slice_in_dim(slab, (1 - c) * own, own, 0))
    gauss_theirs = swap_cores(gauss)
    sketch = sketch_rows(meta, slab, slab_theirs, gauss, gauss_theirs)

    l_got = swap_cores(l_send)
    got = swap(l_keep[2:4] + l_got[2:4], near)
    low = (l_keep[0] + l_got[0]) + got[0]
    low = low + swap((l_keep[1] + l_got[1]) + got[1], far)
    columns = lower_layout(share)
    spread, n = [], 0
    for count in columns:
        spread.append(jnp.pad(low[n:n + count], ((0, NBLK - count), (0, 0), (0, 0))))
        n += count
    low = jnp.stack(spread)
    for s in range(tops):
        bit = (r >> (bits - 1 - s)) & 1
        halves = low.reshape((2, low.shape[0] // 2) + low.shape[1:])
        away = lax.dynamic_index_in_dim(halves, 1 - bit, 0, keepdims=False)
        stay = lax.dynamic_index_in_dim(halves, bit, 0, keepdims=False)
        low = stay + swap(away, (bits - 1 - s,) * 2)
    low_rows = low[0].transpose(1, 0, 2).reshape(share, K)

    factor_rows, up_rows = solve(meta, sketch, block_inverses, (total, piece1, piece2, piece3), share)
    diagonal = (r * 2 + c) * share // BLK
    column = lax.broadcasted_iota(jnp.int32, (share, K), 1) // BLK
    return factor_rows, jnp.where(column > diagonal, up_rows, low_rows)


def solution(mesh):
    return jax.shard_map(
        on_device,
        mesh=mesh,
        in_specs=(P("row", "col"), P("col", None), P(), P()),
        out_specs=(P(("row", "col"), None), P(("row", "col"), None)),
        check_vma=False,
    )
```

```python
import jax
import jax.numpy as jnp
from jax import lax
from jax.experimental import pallas as pl
from jax.experimental.pallas import tpu as pltpu
from jax.sharding import PartitionSpec as P

K = 1024
BLK = 128
NBLK = K // BLK
WIDE = 2 * BLK
NWIDE = K // WIDE
SHARD_ROWS = 2048
PIV_MOST = 128
PICKS = 2 * PIV_MOST
SUB = 16
UPPER = [(i, j) for i in range(NBLK) for j in range(i + 1, NBLK)]
F32 = jnp.float32
BF16 = jnp.bfloat16
I16 = jnp.int16
I32 = jnp.int32
MIB = 1 << 20
VMEM = pl.BlockSpec(memory_space=pltpu.VMEM)
SMEM = pl.BlockSpec(memory_space=pltpu.SMEM)
HBM = pl.BlockSpec(memory_space=pltpu.HBM)


def dot(a, b, dims=((1,), (0,))):
    return lax.dot_general(a, b, (dims, ((), ())), preferred_element_type=F32)


def split(a):
    high = a.astype(BF16)
    return high, (a - high.astype(F32)).astype(BF16)


def product(a, b):
    (ah, al), (bh, bl) = split(a), split(b)
    return dot(ah, bh) + (dot(al, bh) + dot(ah, bl))


def quarter_slot(gx, gy, x, y, c):
    dx, dy = gx ^ x, gy ^ y
    return jnp.where(c == 0, dx * 2 + dy, dy * 2 + dx)


class Copies:
    def __init__(self, source, target, sems):
        count = sems.shape[0]
        rows = target.shape[0] // count
        self.parts = [
            pltpu.make_async_copy(source.at[pl.ds(t * rows, rows)], target.at[pl.ds(t * rows, rows)], sems.at[t])
            for t in range(count)
        ]

    def start(self):
        for part in self.parts:
            part.start()

    def wait(self):
        for part in self.parts:
            part.wait()


def lower_layout(share):
    tops = K // (8 * share)
    return [-(-((z + 1) * 8 * share) // BLK) for z in range(tops)]


def by_core(row, share):
    count = row.shape[1] // (2 * share)
    return jnp.concatenate(
        [row[:, (2 * k + core) * share:(2 * k + core + 1) * share] for core in range(2) for k in range(count)], axis=1)


def pick_kernel(share, meta, piv, slab, packed, place, away, sem):
    r, c = meta[0], meta[1]
    part = SHARD_ROWS // 8
    copies = [
        pltpu.make_async_copy(
            slab.at[pl.ds(pl.multiple_of((1 - c) * SHARD_ROWS + t * part, part), part)],
            away.at[pl.ds(t * part, part)], sem.at[t])
        for t in range(8)
    ]
    for copy in copies:
        copy.start()
    half = lax.broadcasted_iota(I32, (8, K), 0)
    local = by_core(piv[...], share) - (r * (2 * SHARD_ROWS) + half * SHARD_ROWS)
    inside = (local >= 0) & (local < SHARD_ROWS) & (half < 2)
    earlier = lax.broadcasted_iota(I32, (K, K), 0) < lax.broadcasted_iota(I32, (K, K), 1)
    rank = dot(jnp.where(inside, 1.0, 0.0).astype(BF16), jnp.where(earlier, 1.0, 0.0).astype(BF16))
    rank = jnp.where(inside, rank, -1.0)
    order = lax.broadcasted_iota(I32, (PIV_MOST, K), 0).astype(F32)
    rows = lax.broadcasted_iota(I32, (PIV_MOST, SHARD_ROWS), 1).astype(F32)
    for b in range(2):
        hit = rank[b:b + 1, :] == order
        one = jnp.where(hit, 1.0, 0.0).astype(BF16)
        for core in range(2):
            place[core, pl.ds(b * PIV_MOST, PIV_MOST), :] = one[:, core * (K // 2):(core + 1) * (K // 2)]
        row = jnp.sum(jnp.where(hit, local[b:b + 1, :].astype(F32), 0.0), axis=1, keepdims=True)
        part = dot(jnp.where(rows == row, 1.0, 0.0).astype(BF16), slab[pl.ds(b * SHARD_ROWS, SHARD_ROWS), :])
        packed[pl.ds(b * PIV_MOST, PIV_MOST), :] = part.astype(BF16)
    for copy in copies:
        copy.wait()


def pick(meta, piv, slab, share):
    depth = slab.shape[1]
    return pl.pallas_call(
        lambda *refs: pick_kernel(share, *refs),
        out_shape=(
            jax.ShapeDtypeStruct((PICKS, depth), BF16),
            jax.ShapeDtypeStruct((2, PICKS, K // 2), BF16),
            jax.ShapeDtypeStruct((SHARD_ROWS, depth), BF16),
        ),
        in_specs=[SMEM, VMEM, VMEM],
        out_specs=(VMEM, VMEM, HBM),
        scratch_shapes=[pltpu.SemaphoreType.DMA((8,))],
        compiler_params=pltpu.CompilerParams(vmem_limit_bytes=28 * MIB),
        cost_estimate=pl.CostEstimate(flops=4 * 10**9, bytes_accessed=14 * MIB, transcendentals=0),
        name="pick_pivot_rows",
    )(meta, piv, slab)


def pivot_kernel(share, meta, place, packed, packed_theirs, gauss, gauss_theirs,
                 u_keep, u_send, l_keep, l_send, code_v, power_v, u_scr, l_scr):
    r, c = meta[0], meta[1]
    x, y = r & 1, (r >> 1) & 1
    spread = [dot(place[c], p[...], ((0,), (0,))).astype(BF16) for p in (packed, packed_theirs)]
    rows = dot(spread[0], gauss[...]) + dot(spread[1], gauss_theirs[...])
    lane = lax.broadcasted_iota(I32, (K // 2, BLK), 1)
    powers = jnp.zeros((K // 2, BLK), F32)
    for j in range(NBLK):
        part = rows[:, j * BLK:(j + 1) * BLK]
        most = jnp.max(jnp.abs(part), axis=1, keepdims=True)
        power = jnp.where(most > 0.0, jnp.ceil(jnp.log2(jnp.maximum(most, 1e-30)) + 0.001), 0.0)
        code = jnp.floor(part * jnp.exp2(15.0 - power) + 0.5)
        code = jnp.clip(code, -32767.0, 32767.0)
        code_v[:, pl.ds(j * BLK, BLK)] = code.astype(I32).astype(I16)
        powers = jnp.where(lane == j, power, powers)
    power_v[...] = powers

    columns = lower_layout(share)
    lane = lax.broadcasted_iota(I32, (SUB, BLK), 1)
    lane_l = lax.broadcasted_iota(I32, (share, BLK), 1)
    for quarter in range(4):
        gy, gx = quarter >> 1, quarter & 1
        slot = quarter_slot(gx, gy, x, y, c)
        tail = jnp.zeros((SUB, BLK), F32)
        for n, (i, j) in enumerate(UPPER):
            at = pl.ds(i * (BLK // 2) + quarter * SUB, SUB)
            u_scr[slot, n] = code_v[at, pl.ds(j * BLK, BLK)]
            tail = jnp.where(lane == n, power_v[at, j:j + 1], tail)
        u_scr[slot, len(UPPER)] = tail.astype(I32).astype(I16)
        n = 0
        tail = jnp.zeros((share, BLK), F32)
        for z, count in enumerate(columns):
            at = pl.ds((z * 4 + quarter) * share, share)
            for j in range(count):
                l_scr[slot, n] = code_v[at, pl.ds(j * BLK, BLK)].astype(l_scr.dtype)
                tail = jnp.where(lane_l == z * NBLK + j, power_v[at, j:j + 1], tail)
                n += 1
        l_scr[slot, n] = tail.astype(I32).astype(l_scr.dtype)
    u_keep[...] = u_scr[0:2]
    u_send[...] = u_scr[2:4]
    l_keep[...] = l_scr[0:2]
    l_send[...] = l_scr[2:4]


def pivot_rows(meta, place, packed, packed_theirs, gauss, gauss_theirs, share):
    units = sum(lower_layout(share)) + 1
    u_shape = (len(UPPER) + 1, SUB, BLK)
    l_shape = (units, share, BLK)
    l_type = I16 if share % SUB == 0 else I32
    u_out = jax.ShapeDtypeStruct((2,) + u_shape, I16)
    l_out = jax.ShapeDtypeStruct((2,) + l_shape, l_type)
    return pl.pallas_call(
        lambda *refs: pivot_kernel(share, *refs),
        out_shape=(u_out, u_out, l_out, l_out),
        in_specs=[SMEM] + [VMEM] * 5,
        out_specs=(VMEM,) * 4,
        scratch_shapes=[
            pltpu.VMEM((K // 2, K), I16),
            pltpu.VMEM((K // 2, BLK), F32),
            pltpu.VMEM((4,) + u_shape, I16),
            pltpu.VMEM((4,) + l_shape, l_type),
        ],
        compiler_params=pltpu.CompilerParams(vmem_limit_bytes=32 * MIB),
        cost_estimate=pl.CostEstimate(flops=3 * 10**9, bytes_accessed=8 * MIB, transcendentals=0),
        name="pivot_rows",
    )(meta, place, packed, packed_theirs, gauss, gauss_theirs)


def sketch_kernel(part, meta, slab, theirs, gauss, gauss_theirs, later, out, mark, theirs_v, sems):
    rows = out.shape[0]
    tile = theirs_v.shape[1]
    steps = rows // tile
    here = [part * rows + t * tile for t in range(steps)]
    loads = [Copies(theirs.at[pl.ds(here[t], tile)], theirs_v.at[t], sems.at[t]) for t in range(steps)]
    for copy in loads:
        copy.start()
    mark[...] = jnp.zeros_like(mark)
    for t in range(steps):
        mine = pl.ds(pl.multiple_of(meta[1] * theirs.shape[0] + here[t], tile), tile)
        total = dot(slab[mine, :], gauss[...])
        loads[t].wait()
        high, low = split(total + dot(theirs_v[t], gauss_theirs[...]))
        for s in range(NWIDE):
            cols = slice(s * WIDE, (s + 1) * WIDE)
            out[pl.ds(t * tile, tile), pl.ds(2 * s * WIDE, WIDE)] = high[:, cols]
            out[pl.ds(t * tile, tile), pl.ds((2 * s + 1) * WIDE, WIDE)] = low[:, cols]


def sketch_rows(meta, slab, theirs, gauss, gauss_theirs, part, parts, later):
    rows, depth = theirs.shape
    tile = 512
    steps = rows // parts // tile
    return pl.pallas_call(
        lambda *refs: sketch_kernel(part, *refs),
        out_shape=(jax.ShapeDtypeStruct((rows // parts, 2 * K), BF16), jax.ShapeDtypeStruct((SUB, BLK), I16)),
        in_specs=[SMEM, VMEM, HBM, VMEM, VMEM, HBM],
        out_specs=(VMEM, VMEM),
        scratch_shapes=[pltpu.VMEM((steps, tile, depth), BF16), pltpu.SemaphoreType.DMA((steps, 4))],
        compiler_params=pltpu.CompilerParams(vmem_limit_bytes=32 * MIB),
        cost_estimate=pl.CostEstimate(
            flops=4 * rows * depth * K // parts, bytes_accessed=20 * MIB // parts, transcendentals=0),
        name="sketch_rows",
    )(meta, slab, theirs, gauss, gauss_theirs, later)


def store_three(weights, row, cols, value):
    high, low = split(value)
    weights[pl.ds(row, WIDE), cols] = high
    weights[pl.ds(row + WIDE, WIDE), cols] = high
    weights[pl.ds(row + 2 * WIDE, WIDE), cols] = low


def prepare(share, r, c, inverses, pieces, low, own_rows, coupling, weights):
    x, y = r & 1, (r >> 1) & 1
    lane = lax.broadcasted_iota(I32, (SUB, BLK), 1)
    coupling[...] = jnp.zeros_like(coupling)
    slot = 0
    chunk = min(SUB, share)
    for piece in pieces:
        for k in range(piece.shape[0]):
            gc = c ^ (slot >> 2)
            high, less = (slot >> 1) & 1, slot & 1
            dx, dy = jnp.where(gc == 0, high, less), jnp.where(gc == 0, less, high)
            quarter = (y ^ dy) * 2 + (x ^ dx)
            tail = piece[k, len(UPPER)].astype(I32).astype(F32)
            for i in range(NBLK - 1):
                starts = []
                for part in range(SUB // chunk):
                    s = i * (BLK // 2) + quarter * SUB + part * chunk
                    owner = lax.div(s, share)
                    starts.append(pl.multiple_of((owner * 2 + gc) * share + (s - owner * share), 8))
                for n, (row_block, j) in enumerate(UPPER):
                    if row_block != i:
                        continue
                    scale = jnp.exp2(tail[:, n:n + 1] - 15.0) * (-1.0 / K**0.5)
                    value = piece[k, n].astype(I32).astype(F32) * scale
                    for part in range(SUB // chunk):
                        coupling[pl.ds(starts[part], chunk), pl.ds(j * BLK, BLK)] = (
                            value[part * chunk:(part + 1) * chunk])
            slot += 1

    own = (r * 2 + c) * share
    up = coupling[pl.ds(pl.multiple_of(own, 8), share), :] * (-(K**0.5))
    tail = low[NBLK].astype(I32)
    place = lax.broadcasted_iota(I32, (share, BLK), 1) - (r >> 2) * NBLK
    diagonal = lax.div(own, BLK)
    for j in range(NBLK):
        power = jnp.sum(jnp.where(place == j, tail, 0), axis=1, keepdims=True).astype(F32)
        value = low[j].astype(I32).astype(F32) * jnp.exp2(power - 15.0)
        cols = pl.ds(j * BLK, BLK)
        own_rows[:, cols] = jnp.where(j > diagonal, up[:, j * BLK:(j + 1) * BLK], value)

    for s in range(NWIDE):
        first, second = inverses[2 * s], inverses[2 * s + 1]
        link = coupling[pl.ds(2 * s * BLK, BLK), pl.ds((2 * s + 1) * BLK, BLK)]
        corner = product(first, product(link, second))
        block = jnp.concatenate([
            jnp.concatenate([first, corner], axis=1),
            jnp.concatenate([jnp.zeros_like(first), second], axis=1)], axis=0)
        cols = pl.ds(s * WIDE, WIDE)
        store_three(weights, 0, cols, block)
        if s > 0:
            turned = product(coupling[pl.ds(0, s * WIDE), cols], block)
            for e in range(s):
                store_three(weights, 3 * (e + 1) * WIDE, cols, turned[e * WIDE:(e + 1) * WIDE])


def solve_kernel(share, parts, meta, *refs):
    sketches, refs = refs[:parts], refs[parts:]
    (inverses, p0, p1, p2, p3, low, out, own_rows,
     coupling, weights, earlier, pair_v, out_v, in_sems, out_sems) = refs
    tile = out_v.shape[1]
    each = sketches[0].shape[0] // tile
    steps = each * parts

    def start_in(step):
        slot = lax.rem(step, 2)
        for part in range(parts):
            @pl.when(lax.div(step, each) == part)
            def _():
                where = pl.ds(pl.multiple_of((step - part * each) * tile, tile), tile)
                pltpu.make_async_copy(sketches[part].at[where], pair_v.at[slot], in_sems.at[slot]).start()

    def copy_out(step):
        slot = lax.rem(step, 2)
        where = pl.ds(pl.multiple_of(step * tile, tile), tile)
        return pltpu.make_async_copy(out_v.at[slot], out.at[where], out_sems.at[slot])

    start_in(jnp.int32(0))
    start_in(jnp.int32(1))
    prepare(share, meta[0], meta[1], inverses, (p0, p1, p2, p3), low, own_rows, coupling, weights)
    sub = 256

    @pl.loop(0, steps)
    def _(step):
        slot = lax.rem(step, 2)

        @pl.when(step >= 2)
        def _():
            copy_out(step - 2).wait()

        pltpu.make_async_copy(sketches[0].at[pl.ds(0, tile)], pair_v.at[slot], in_sems.at[slot]).wait()
        for s in range(NWIDE):
            cols = pl.ds(s * WIDE, WIDE)
            for q in range(tile // sub):
                here = pl.ds(q * sub, sub)
                pair = pair_v[slot, here, pl.ds(2 * s * WIDE, 2 * WIDE)]
                high = pair_v[slot, here, pl.ds(2 * s * WIDE, WIDE)]
                acc = dot(pair, weights[pl.ds(0, 2 * WIDE), cols]) + dot(high, weights[pl.ds(2 * WIDE, WIDE), cols])
                if s > 0:
                    depth = 3 * s * WIDE
                    acc = acc + dot(earlier[here, pl.ds(0, depth)], weights[pl.ds(3 * WIDE, depth), cols])
                out_v[slot, here, cols] = acc
                if s < NWIDE - 1:
                    high, low_part = split(acc)
                    to = 3 * s * WIDE
                    earlier[here, pl.ds(to, WIDE)] = high
                    earlier[here, pl.ds(to + WIDE, WIDE)] = low_part
                    earlier[here, pl.ds(to + 2 * WIDE, WIDE)] = high
        copy_out(step).start()

        @pl.when(step + 2 < steps)
        def _():
            start_in(step + 2)

    for step in range(2):
        copy_out(jnp.int32(steps - 2 + step)).wait()


def solve(meta, sketches, inverses, pieces, low, share):
    parts = len(sketches)
    rows = sum(s.shape[0] for s in sketches)
    tile = 512
    return pl.pallas_call(
        lambda *refs: solve_kernel(share, parts, *refs),
        out_shape=(jax.ShapeDtypeStruct((rows, K), F32), jax.ShapeDtypeStruct((share, K), F32)),
        in_specs=[SMEM] + [HBM] * parts + [VMEM] * (2 + len(pieces)),
        out_specs=(HBM, VMEM),
        scratch_shapes=[
            pltpu.VMEM((K, K), F32),
            pltpu.VMEM((3 * K, K), BF16),
            pltpu.VMEM((tile, 3 * (NWIDE - 1) * WIDE), BF16),
            pltpu.VMEM((2, tile, 2 * K), BF16),
            pltpu.VMEM((2, tile, K), F32),
            pltpu.SemaphoreType.DMA((2,)),
            pltpu.SemaphoreType.DMA((2,)),
        ],
        compiler_params=pltpu.CompilerParams(vmem_limit_bytes=58 * MIB),
        cost_estimate=pl.CostEstimate(flops=8 * 10**9, bytes_accessed=20 * MIB, transcendentals=0),
        name="blocked_solve",
    )(meta, *sketches, inverses, *pieces, low)


def after(value, *others):
    return lax.optimization_barrier((value,) + others)[0]


def on_device(slab, gauss, pivots, block_inverses):
    rows = lax.axis_size("row")
    cols = lax.axis_size("col")
    bits = rows.bit_length() - 1
    tops = bits - 2
    share = K // (rows * cols)
    r, c = lax.axis_index("row"), lax.axis_index("col")
    meta = jnp.stack([r, c]).astype(I32)

    def swap(value, bit_of):
        perm = [(2 * i + k, 2 * (i ^ (1 << bit_of[k])) + k) for i in range(rows) for k in range(2)]
        return lax.ppermute(value, ("row", "col"), perm)

    def swap_cores(value):
        return lax.ppermute(value, "col", [(0, 1), (1, 0)])

    near, far = (0, 1), (1, 0)
    climb = [(2 + s, 2 + (s + 1) % tops) for s in range(tops)]

    gauss_theirs = swap_cores(gauss)
    packed, place, slab_away = pick(meta, pivots.reshape(1, K), slab, share)
    packed_theirs = swap_cores(packed + gauss_theirs[:1] * 0)
    slab_away, mark = lax.optimization_barrier((slab_away, packed_theirs[:SUB, :BLK]))
    slab_theirs = swap_cores(slab_away)
    u_keep, u_send, l_keep, l_send = pivot_rows(
        meta, place, packed, packed_theirs, gauss, gauss_theirs, share)


    parts = 2

    def sketch_part(part, later):
        return sketch_rows(meta, slab, slab_theirs, gauss, gauss_theirs, part, parts, later)

    size, l_shape = u_keep[0].size // BLK, l_keep.shape[1:]

    def join(upper, lower):
        count = upper.shape[0]
        return jnp.concatenate(
            [upper.reshape(count, -1, BLK), lower.astype(I16).reshape(count, -1, BLK)], axis=1)

    keep, send = join(u_keep, l_keep), join(u_send, l_send)
    sketch, mark = sketch_part(0, mark)
    sketches = [sketch]
    got = swap(send, near) + mark[:1]
    send = keep[1:2] + got[1:2]
    kept = keep[0:1] + got[0:1]
    sketch, mark = sketch_part(1, send)
    sketches.append(sketch)
    kept = kept + (swap(send, far) + mark[:1])
    total = kept[:, :size].reshape(u_keep[:1].shape)
    low = kept[0, size:].reshape(l_shape)
    spread, n = [], 0
    for count in lower_layout(share):
        block = jnp.pad(low[n:n + count], ((0, NBLK - count), (0, 0), (0, 0)))
        spread.append(jnp.concatenate([block, low[-1:]], axis=0))
        n += count
    spread = jnp.stack(spread)
    order = []
    for k in range(1 << tops):
        at = r >> 2
        for s in range(tops):
            if (k >> (tops - 1 - s)) & 1:
                at = at ^ jnp.where(c == 0, 1 << (climb[s][0] - 2), 1 << (climb[s][1] - 2))
        order.append(lax.dynamic_index_in_dim(spread, at, 0, keepdims=False))
    low = jnp.stack(order)
    for bit_of in climb:
        half = low.shape[0] // 2
        both = jnp.concatenate([total.reshape(size, BLK), low[half:].reshape(-1, BLK)], axis=0)
        got = swap(both, bit_of)
        total = total + got[:size].reshape(total.shape)
        low = low[:half] + got[size:].reshape(low[:half].shape)
    piece1 = swap(total, far)
    pair = jnp.concatenate([total, piece1], axis=0)
    piece2 = swap(pair, near)
    piece3 = swap_cores(jnp.concatenate([pair, piece2], axis=0))
    return solve(meta, sketches, block_inverses, (total, piece1, piece2, piece3), low[0], share)


def solution(mesh):
    return jax.shard_map(
        on_device,
        mesh=mesh,
        in_specs=(P("row", "col"), P("col", None), P(), P()),
        out_specs=(P(("row", "col"), None), P(("row", "col"), None)),
        check_vma=False,
    )
```

```python
import jax
import jax.numpy as jnp
from jax import lax
from jax.experimental import pallas as pl
from jax.experimental.pallas import tpu as pltpu
from jax.sharding import PartitionSpec as P

K = 1024
BLK = 128
NBLK = K // BLK
WIDE = 2 * BLK
NWIDE = K // WIDE
SHARD_ROWS = 2048
PIV_MOST = 128
PICKS = 2 * PIV_MOST
SUB = 16
UPPER = [(i, j) for i in range(NBLK) for j in range(i + 1, NBLK)]
F32 = jnp.float32
BF16 = jnp.bfloat16
I16 = jnp.int16
I32 = jnp.int32
MIB = 1 << 20
VMEM = pl.BlockSpec(memory_space=pltpu.VMEM)
SMEM = pl.BlockSpec(memory_space=pltpu.SMEM)
HBM = pl.BlockSpec(memory_space=pltpu.HBM)


def dot(a, b, dims=((1,), (0,))):
    return lax.dot_general(a, b, (dims, ((), ())), preferred_element_type=F32)


def split(a):
    high = a.astype(BF16)
    return high, (a - high.astype(F32)).astype(BF16)


def product(a, b):
    (ah, al), (bh, bl) = split(a), split(b)
    return dot(ah, bh) + (dot(al, bh) + dot(ah, bl))


def quarter_slot(gx, gy, x, y, c):
    dx, dy = gx ^ x, gy ^ y
    return jnp.where(c == 0, dx * 2 + dy, dy * 2 + dx)


class Copies:
    def __init__(self, source, target, sems):
        count = sems.shape[0]
        rows = target.shape[0] // count
        self.parts = [
            pltpu.make_async_copy(source.at[pl.ds(t * rows, rows)], target.at[pl.ds(t * rows, rows)], sems.at[t])
            for t in range(count)
        ]

    def start(self):
        for part in self.parts:
            part.start()

    def wait(self):
        for part in self.parts:
            part.wait()


def lower_layout(share):
    tops = K // (8 * share)
    return [-(-((z + 1) * 8 * share) // BLK) for z in range(tops)]


def by_core(row, share):
    count = row.shape[1] // (2 * share)
    return jnp.concatenate(
        [row[:, (2 * k + core) * share:(2 * k + core + 1) * share] for core in range(2) for k in range(count)], axis=1)


def pick_kernel(share, meta, piv, slab, packed, place, away, sem):
    r, c = meta[0], meta[1]
    part = SHARD_ROWS // 8
    copies = [
        pltpu.make_async_copy(
            slab.at[pl.ds(pl.multiple_of((1 - c) * SHARD_ROWS + t * part, part), part)],
            away.at[pl.ds(t * part, part)], sem.at[t])
        for t in range(8)
    ]
    for copy in copies:
        copy.start()
    half = lax.broadcasted_iota(I32, (8, K), 0)
    local = by_core(piv[...], share) - (r * (2 * SHARD_ROWS) + half * SHARD_ROWS)
    inside = (local >= 0) & (local < SHARD_ROWS) & (half < 2)
    earlier = lax.broadcasted_iota(I32, (K, K), 0) < lax.broadcasted_iota(I32, (K, K), 1)
    rank = dot(jnp.where(inside, 1.0, 0.0).astype(BF16), jnp.where(earlier, 1.0, 0.0).astype(BF16))
    rank = jnp.where(inside, rank, -1.0)
    order = lax.broadcasted_iota(I32, (PIV_MOST, K), 0).astype(F32)
    rows = lax.broadcasted_iota(I32, (PIV_MOST, SHARD_ROWS), 1).astype(F32)
    for b in range(2):
        hit = rank[b:b + 1, :] == order
        one = jnp.where(hit, 1.0, 0.0).astype(BF16)
        for core in range(2):
            place[core, pl.ds(b * PIV_MOST, PIV_MOST), :] = one[:, core * (K // 2):(core + 1) * (K // 2)]
        row = jnp.sum(jnp.where(hit, local[b:b + 1, :].astype(F32), 0.0), axis=1, keepdims=True)
        part = dot(jnp.where(rows == row, 1.0, 0.0).astype(BF16), slab[pl.ds(b * SHARD_ROWS, SHARD_ROWS), :])
        packed[pl.ds(b * PIV_MOST, PIV_MOST), :] = part.astype(BF16)
    for copy in copies:
        copy.wait()


def pick(meta, piv, slab, share):
    depth = slab.shape[1]
    return pl.pallas_call(
        lambda *refs: pick_kernel(share, *refs),
        out_shape=(
            jax.ShapeDtypeStruct((PICKS, depth), BF16),
            jax.ShapeDtypeStruct((2, PICKS, K // 2), BF16),
            jax.ShapeDtypeStruct((SHARD_ROWS, depth), BF16),
        ),
        in_specs=[SMEM, VMEM, VMEM],
        out_specs=(VMEM, VMEM, HBM),
        scratch_shapes=[pltpu.SemaphoreType.DMA((8,))],
        compiler_params=pltpu.CompilerParams(vmem_limit_bytes=22 * MIB),
        cost_estimate=pl.CostEstimate(flops=4 * 10**9, bytes_accessed=14 * MIB, transcendentals=0),
        name="pick_pivot_rows",
    )(meta, piv, slab)


def pivot_kernel(share, meta, place, packed, packed_theirs, gauss, gauss_theirs,
                 u_keep, u_send, l_keep, l_send, code_v, power_v, u_scr, l_scr):
    r, c = meta[0], meta[1]
    x, y = r & 1, (r >> 1) & 1
    rows = dot(packed[...], gauss[...]) + dot(packed_theirs[...], gauss_theirs[...])
    lane = lax.broadcasted_iota(I32, (PICKS, BLK), 1)
    powers = jnp.zeros((PICKS, BLK), F32)
    highs, lows = [], []
    for j in range(NBLK):
        part = rows[:, j * BLK:(j + 1) * BLK]
        most = jnp.max(jnp.abs(part), axis=1, keepdims=True)
        power = jnp.where(most > 0.0, jnp.ceil(jnp.log2(jnp.maximum(most, 1e-30)) + 0.001), 0.0)
        code = jnp.floor(part * jnp.exp2(15.0 - power) + 0.5)
        code = jnp.clip(code, -32767.0, 32767.0)
        high = jnp.floor(code * (1.0 / 256.0))
        highs.append(high.astype(BF16))
        lows.append((code - 256.0 * high).astype(BF16))
        powers = jnp.where(lane == j, power, powers)
    spread = dot(place[c], jnp.concatenate(highs + lows + [powers.astype(BF16)], axis=1), ((0,), (0,)))
    code_v[...] = (spread[:, :K] * 256.0 + spread[:, K:2 * K]).astype(I32).astype(I16)
    power_v[...] = spread[:, 2 * K:]

    columns = lower_layout(share)
    lane = lax.broadcasted_iota(I32, (SUB, BLK), 1)
    lane_l = lax.broadcasted_iota(I32, (share, BLK), 1)
    for quarter in range(4):
        gy, gx = quarter >> 1, quarter & 1
        slot = quarter_slot(gx, gy, x, y, c)
        tail = jnp.zeros((SUB, BLK), F32)
        for n, (i, j) in enumerate(UPPER):
            at = pl.ds(i * (BLK // 2) + quarter * SUB, SUB)
            u_scr[slot, n] = code_v[at, pl.ds(j * BLK, BLK)]
            tail = jnp.where(lane == n, power_v[at, j:j + 1], tail)
        u_scr[slot, len(UPPER)] = tail.astype(I32).astype(I16)
        n = 0
        tail = jnp.zeros((share, BLK), F32)
        for z, count in enumerate(columns):
            at = pl.ds((z * 4 + quarter) * share, share)
            for j in range(count):
                l_scr[slot, n] = code_v[at, pl.ds(j * BLK, BLK)].astype(l_scr.dtype)
                tail = jnp.where(lane_l == z * NBLK + j, power_v[at, j:j + 1], tail)
                n += 1
        l_scr[slot, n] = tail.astype(I32).astype(l_scr.dtype)
    u_keep[...] = u_scr[0:2]
    u_send[...] = u_scr[2:4]
    l_keep[...] = l_scr[0:2]
    l_send[...] = l_scr[2:4]


def pivot_rows(meta, place, packed, packed_theirs, gauss, gauss_theirs, share):
    units = sum(lower_layout(share)) + 1
    u_shape = (len(UPPER) + 1, SUB, BLK)
    l_shape = (units, share, BLK)
    l_type = I16 if share % SUB == 0 else I32
    u_out = jax.ShapeDtypeStruct((2,) + u_shape, I16)
    l_out = jax.ShapeDtypeStruct((2,) + l_shape, l_type)
    return pl.pallas_call(
        lambda *refs: pivot_kernel(share, *refs),
        out_shape=(u_out, u_out, l_out, l_out),
        in_specs=[SMEM] + [VMEM] * 5,
        out_specs=(VMEM,) * 4,
        scratch_shapes=[
            pltpu.VMEM((K // 2, K), I16),
            pltpu.VMEM((K // 2, BLK), F32),
            pltpu.VMEM((4,) + u_shape, I16),
            pltpu.VMEM((4,) + l_shape, l_type),
        ],
        compiler_params=pltpu.CompilerParams(vmem_limit_bytes=24 * MIB),
        cost_estimate=pl.CostEstimate(flops=3 * 10**9, bytes_accessed=8 * MIB, transcendentals=0),
        name="pivot_rows",
    )(meta, place, packed, packed_theirs, gauss, gauss_theirs)


def sketch_kernel(part, meta, slab, theirs, gauss, gauss_theirs, later, out, mark, theirs_v, sems):
    rows = out.shape[0]
    tile = theirs_v.shape[1]
    steps = rows // tile
    here = [part * rows + t * tile for t in range(steps)]
    loads = [Copies(theirs.at[pl.ds(here[t], tile)], theirs_v.at[t], sems.at[t]) for t in range(steps)]
    for copy in loads:
        copy.start()
    mark[...] = jnp.zeros_like(mark)
    for t in range(steps):
        mine = pl.ds(pl.multiple_of(meta[1] * theirs.shape[0] + here[t], tile), tile)
        total = dot(slab[mine, :], gauss[...])
        loads[t].wait()
        high, low = split(total + dot(theirs_v[t], gauss_theirs[...]))
        for s in range(NWIDE):
            cols = slice(s * WIDE, (s + 1) * WIDE)
            out[pl.ds(t * tile, tile), pl.ds(2 * s * WIDE, WIDE)] = high[:, cols]
            out[pl.ds(t * tile, tile), pl.ds((2 * s + 1) * WIDE, WIDE)] = low[:, cols]


def sketch_rows(meta, slab, theirs, gauss, gauss_theirs, part, parts, later):
    rows, depth = theirs.shape
    tile = 512
    steps = rows // parts // tile
    return pl.pallas_call(
        lambda *refs: sketch_kernel(part, *refs),
        out_shape=(jax.ShapeDtypeStruct((rows // parts, 2 * K), BF16), jax.ShapeDtypeStruct((SUB, BLK), I16)),
        in_specs=[SMEM, VMEM, HBM, VMEM, VMEM, HBM],
        out_specs=(VMEM, VMEM),
        scratch_shapes=[pltpu.VMEM((steps, tile, depth), BF16), pltpu.SemaphoreType.DMA((steps, 4))],
        compiler_params=pltpu.CompilerParams(vmem_limit_bytes=24 * MIB),
        cost_estimate=pl.CostEstimate(
            flops=4 * rows * depth * K // parts, bytes_accessed=20 * MIB // parts, transcendentals=0),
        name="sketch_rows",
    )(meta, slab, theirs, gauss, gauss_theirs, later)


def store_three(weights, row, cols, value):
    high, low = split(value)
    weights[pl.ds(row, WIDE), cols] = high
    weights[pl.ds(row + WIDE, WIDE), cols] = high
    weights[pl.ds(row + 2 * WIDE, WIDE), cols] = low


def prepare(share, r, c, inverses, pieces, low, own_rows, coupling, weights):
    x, y = r & 1, (r >> 1) & 1
    lane = lax.broadcasted_iota(I32, (SUB, BLK), 1)
    coupling[...] = jnp.zeros_like(coupling)
    slot = 0
    chunk = min(SUB, share)
    for piece in pieces:
        for k in range(piece.shape[0]):
            gc = c ^ (slot >> 2)
            high, less = (slot >> 1) & 1, slot & 1
            dx, dy = jnp.where(gc == 0, high, less), jnp.where(gc == 0, less, high)
            quarter = (y ^ dy) * 2 + (x ^ dx)
            tail = piece[k, len(UPPER)].astype(I32).astype(F32)
            for i in range(NBLK - 1):
                starts = []
                for part in range(SUB // chunk):
                    s = i * (BLK // 2) + quarter * SUB + part * chunk
                    owner = lax.div(s, share)
                    starts.append(pl.multiple_of((owner * 2 + gc) * share + (s - owner * share), 8))
                for n, (row_block, j) in enumerate(UPPER):
                    if row_block != i:
                        continue
                    scale = jnp.exp2(tail[:, n:n + 1] - 15.0) * (-1.0 / K**0.5)
                    value = piece[k, n].astype(I32).astype(F32) * scale
                    for part in range(SUB // chunk):
                        coupling[pl.ds(starts[part], chunk), pl.ds(j * BLK, BLK)] = (
                            value[part * chunk:(part + 1) * chunk])
            slot += 1

    own = (r * 2 + c) * share
    up = coupling[pl.ds(pl.multiple_of(own, 8), share), :] * (-(K**0.5))
    tail = low[NBLK].astype(I32)
    place = lax.broadcasted_iota(I32, (share, BLK), 1) - (r >> 2) * NBLK
    diagonal = lax.div(own, BLK)
    for j in range(NBLK):
        power = jnp.sum(jnp.where(place == j, tail, 0), axis=1, keepdims=True).astype(F32)
        value = low[j].astype(I32).astype(F32) * jnp.exp2(power - 15.0)
        cols = pl.ds(j * BLK, BLK)
        own_rows[:, cols] = jnp.where(j > diagonal, up[:, j * BLK:(j + 1) * BLK], value)

    for s in range(NWIDE):
        first, second = inverses[2 * s], inverses[2 * s + 1]
        link = coupling[pl.ds(2 * s * BLK, BLK), pl.ds((2 * s + 1) * BLK, BLK)]
        corner = product(first, product(link, second))
        block = jnp.concatenate([
            jnp.concatenate([first, corner], axis=1),
            jnp.concatenate([jnp.zeros_like(first), second], axis=1)], axis=0)
        cols = pl.ds(s * WIDE, WIDE)
        store_three(weights, 0, cols, block)
        if s > 0:
            turned = product(coupling[pl.ds(0, s * WIDE), cols], block)
            for e in range(s):
                store_three(weights, 3 * (e + 1) * WIDE, cols, turned[e * WIDE:(e + 1) * WIDE])


def solve_kernel(share, parts, meta, *refs):
    sketches, refs = refs[:parts], refs[parts:]
    (inverses, p0, p1, p2, p3, low, out, own_rows,
     coupling, weights, earlier, pair_v, out_v, in_sems, out_sems) = refs
    tile = out_v.shape[1]
    each = sketches[0].shape[0] // tile
    steps = each * parts

    def start_in(step):
        slot = lax.rem(step, 2)
        for part in range(parts):
            @pl.when(lax.div(step, each) == part)
            def _():
                where = pl.ds(pl.multiple_of((step - part * each) * tile, tile), tile)
                pltpu.make_async_copy(sketches[part].at[where], pair_v.at[slot], in_sems.at[slot]).start()

    def copy_out(step):
        slot = lax.rem(step, 2)
        where = pl.ds(pl.multiple_of(step * tile, tile), tile)
        return pltpu.make_async_copy(out_v.at[slot], out.at[where], out_sems.at[slot])

    start_in(jnp.int32(0))
    start_in(jnp.int32(1))
    prepare(share, meta[0], meta[1], inverses, (p0, p1, p2, p3), low, own_rows, coupling, weights)
    sub = 256

    @pl.loop(0, steps)
    def _(step):
        slot = lax.rem(step, 2)

        @pl.when(step >= 2)
        def _():
            copy_out(step - 2).wait()

        pltpu.make_async_copy(sketches[0].at[pl.ds(0, tile)], pair_v.at[slot], in_sems.at[slot]).wait()
        for s in range(NWIDE):
            cols = pl.ds(s * WIDE, WIDE)
            for q in range(tile // sub):
                here = pl.ds(q * sub, sub)
                pair = pair_v[slot, here, pl.ds(2 * s * WIDE, 2 * WIDE)]
                high = pair_v[slot, here, pl.ds(2 * s * WIDE, WIDE)]
                acc = dot(pair, weights[pl.ds(0, 2 * WIDE), cols]) + dot(high, weights[pl.ds(2 * WIDE, WIDE), cols])
                if s > 0:
                    depth = 3 * s * WIDE
                    acc = acc + dot(earlier[here, pl.ds(0, depth)], weights[pl.ds(3 * WIDE, depth), cols])
                out_v[slot, here, cols] = acc
                if s < NWIDE - 1:
                    high, low_part = split(acc)
                    to = 3 * s * WIDE
                    earlier[here, pl.ds(to, WIDE)] = high
                    earlier[here, pl.ds(to + WIDE, WIDE)] = low_part
                    earlier[here, pl.ds(to + 2 * WIDE, WIDE)] = high
        copy_out(step).start()

        @pl.when(step + 2 < steps)
        def _():
            start_in(step + 2)

    for step in range(2):
        copy_out(jnp.int32(steps - 2 + step)).wait()


def solve(meta, sketches, inverses, pieces, low, share):
    parts = len(sketches)
    rows = sum(s.shape[0] for s in sketches)
    tile = 512
    return pl.pallas_call(
        lambda *refs: solve_kernel(share, parts, *refs),
        out_shape=(jax.ShapeDtypeStruct((rows, K), F32), jax.ShapeDtypeStruct((share, K), F32)),
        in_specs=[SMEM] + [HBM] * parts + [VMEM] * (2 + len(pieces)),
        out_specs=(HBM, VMEM),
        scratch_shapes=[
            pltpu.VMEM((K, K), F32),
            pltpu.VMEM((3 * K, K), BF16),
            pltpu.VMEM((tile, 3 * (NWIDE - 1) * WIDE), BF16),
            pltpu.VMEM((2, tile, 2 * K), BF16),
            pltpu.VMEM((2, tile, K), F32),
            pltpu.SemaphoreType.DMA((2,)),
            pltpu.SemaphoreType.DMA((2,)),
        ],
        compiler_params=pltpu.CompilerParams(vmem_limit_bytes=52 * MIB),
        cost_estimate=pl.CostEstimate(flops=8 * 10**9, bytes_accessed=20 * MIB, transcendentals=0),
        name="blocked_solve",
    )(meta, *sketches, inverses, *pieces, low)


def after(value, *others):
    return lax.optimization_barrier((value,) + others)[0]


def on_device(slab, gauss, pivots, block_inverses):
    rows = lax.axis_size("row")
    cols = lax.axis_size("col")
    bits = rows.bit_length() - 1
    tops = bits - 2
    share = K // (rows * cols)
    r, c = lax.axis_index("row"), lax.axis_index("col")
    meta = jnp.stack([r, c]).astype(I32)

    def swap(value, bit_of):
        perm = [(2 * i + k, 2 * (i ^ (1 << bit_of[k])) + k) for i in range(rows) for k in range(2)]
        return lax.ppermute(value, ("row", "col"), perm)

    def swap_cores(value):
        return lax.ppermute(value, "col", [(0, 1), (1, 0)])

    near, far = (0, 1), (1, 0)
    climb = [(2 + s, 2 + (s + 1) % tops) for s in range(tops)]

    gauss_theirs = swap_cores(gauss)
    packed, place, slab_away = pick(meta, pivots.reshape(1, K), slab, share)
    packed_theirs = swap_cores(packed + gauss_theirs[:1] * 0)
    slab_away, mark = lax.optimization_barrier((slab_away, packed_theirs[:SUB, :BLK]))
    slab_theirs = swap_cores(slab_away)
    u_keep, u_send, l_keep, l_send = pivot_rows(
        meta, place, packed, packed_theirs, gauss, gauss_theirs, share)


    parts = 2

    def sketch_part(part, later):
        return sketch_rows(meta, slab, slab_theirs, gauss, gauss_theirs, part, parts, later)

    size, l_shape = u_keep[0].size // BLK, l_keep.shape[1:]

    def join(upper, lower):
        count = upper.shape[0]
        return jnp.concatenate(
            [upper.reshape(count, -1, BLK), lower.astype(I16).reshape(count, -1, BLK)], axis=1)

    keep, send = join(u_keep, l_keep), join(u_send, l_send)
    sketch, mark = sketch_part(0, mark)
    sketches = [sketch]
    got = swap(send, near) + mark[:1]
    send = keep[1:2] + got[1:2]
    kept = keep[0:1] + got[0:1]
    sketch, mark = sketch_part(1, send)
    sketches.append(sketch)
    kept = kept + (swap(send, far) + mark[:1])
    total = kept[:, :size].reshape(u_keep[:1].shape)
    low = kept[0, size:].reshape(l_shape)
    spread, n = [], 0
    for count in lower_layout(share):
        block = jnp.pad(low[n:n + count], ((0, NBLK - count), (0, 0), (0, 0)))
        spread.append(jnp.concatenate([block, low[-1:]], axis=0))
        n += count
    spread = jnp.stack(spread)
    order = []
    for k in range(1 << tops):
        at = r >> 2
        for s in range(tops):
            if (k >> (tops - 1 - s)) & 1:
                at = at ^ jnp.where(c == 0, 1 << (climb[s][0] - 2), 1 << (climb[s][1] - 2))
        order.append(lax.dynamic_index_in_dim(spread, at, 0, keepdims=False))
    low = jnp.stack(order)
    for s, bit_of in enumerate(climb):
        got = swap(total, bit_of)
        if s == 0:
            low = after(low, got)
        total = total + got
    got = swap(total, far)
    for bit_of in climb:
        half = low.shape[0] // 2
        low_got = swap(low[half:], bit_of)
        low = low[:half] + low_got
    piece1 = after(got, low_got)
    pair = jnp.concatenate([total, piece1], axis=0)
    piece2 = swap(pair, near)
    piece3 = swap_cores(jnp.concatenate([pair, piece2], axis=0))
    return solve(meta, sketches, block_inverses, (total, piece1, piece2, piece3), low[0], share)


def solution(mesh):
    return jax.shard_map(
        on_device,
        mesh=mesh,
        in_specs=(P("row", "col"), P("col", None), P(), P()),
        out_specs=(P(("row", "col"), None), P(("row", "col"), None)),
        check_vma=False,
    )
```

```python
import jax
import jax.numpy as jnp
from jax import lax
from jax.experimental import pallas as pl
from jax.experimental.pallas import tpu as pltpu
from jax.sharding import PartitionSpec as P

K = 1024
BLK = 128
NBLK = K // BLK
WIDE = 2 * BLK
NWIDE = K // WIDE
SHARD_ROWS = 2048
PIV_MOST = 128
PICKS = 2 * PIV_MOST
PIECE = 256
SUB = 16
UPPER = [(i, j) for i in range(NBLK) for j in range(i + 1, NBLK)]
F32 = jnp.float32
BF16 = jnp.bfloat16
I16 = jnp.int16
I32 = jnp.int32
MIB = 1 << 20
VMEM = pl.BlockSpec(memory_space=pltpu.VMEM)
SMEM = pl.BlockSpec(memory_space=pltpu.SMEM)
HBM = pl.BlockSpec(memory_space=pltpu.HBM)


def dot(a, b, dims=((1,), (0,))):
    return lax.dot_general(a, b, (dims, ((), ())), preferred_element_type=F32)


def split(a):
    high = a.astype(BF16)
    return high, (a - high.astype(F32)).astype(BF16)


def product(a, b):
    (ah, al), (bh, bl) = split(a), split(b)
    return dot(ah, bh) + (dot(al, bh) + dot(ah, bl))


def quarter_slot(gx, gy, x, y, c):
    dx, dy = gx ^ x, gy ^ y
    return jnp.where(c == 0, dx * 2 + dy, dy * 2 + dx)


class Copies:
    def __init__(self, source, target, sems):
        count = sems.shape[0]
        rows = target.shape[0] // count
        self.parts = [
            pltpu.make_async_copy(source.at[pl.ds(t * rows, rows)], target.at[pl.ds(t * rows, rows)], sems.at[t])
            for t in range(count)
        ]

    def start(self):
        for part in self.parts:
            part.start()

    def wait(self):
        for part in self.parts:
            part.wait()


def lower_layout(share):
    tops = K // (8 * share)
    return [-(-((z + 1) * 8 * share) // BLK) for z in range(tops)]


def by_core(row, share):
    count = row.shape[1] // (2 * share)
    return jnp.concatenate(
        [row[:, (2 * k + core) * share:(2 * k + core + 1) * share] for core in range(2) for k in range(count)], axis=1)


def pick_kernel(share, meta, piv, slab, packed, place, away, sem):
    r, c = meta[0], meta[1]
    part = SHARD_ROWS // 8
    copies = [
        pltpu.make_async_copy(
            slab.at[pl.ds(pl.multiple_of((1 - c) * SHARD_ROWS + t * part, part), part)],
            away.at[pl.ds(t * part, part)], sem.at[t])
        for t in range(8)
    ]
    for copy in copies:
        copy.start()
    half = lax.broadcasted_iota(I32, (8, K), 0)
    local = by_core(piv[...], share) - (r * (2 * SHARD_ROWS) + half * SHARD_ROWS)
    inside = (local >= 0) & (local < SHARD_ROWS) & (half < 2)
    earlier = lax.broadcasted_iota(I32, (K, K), 0) < lax.broadcasted_iota(I32, (K, K), 1)
    rank = dot(jnp.where(inside, 1.0, 0.0).astype(BF16), jnp.where(earlier, 1.0, 0.0).astype(BF16))
    rank = jnp.where(inside, rank, -1.0)
    order = lax.broadcasted_iota(I32, (PIV_MOST, K), 0).astype(F32)
    rows = lax.broadcasted_iota(I32, (PIV_MOST, SHARD_ROWS), 1).astype(F32)
    for b in range(2):
        hit = rank[b:b + 1, :] == order
        one = jnp.where(hit, 1.0, 0.0).astype(BF16)
        for core in range(2):
            place[core, pl.ds(b * PIV_MOST, PIV_MOST), :] = one[:, core * (K // 2):(core + 1) * (K // 2)]
        row = jnp.sum(jnp.where(hit, local[b:b + 1, :].astype(F32), 0.0), axis=1, keepdims=True)
        part = dot(jnp.where(rows == row, 1.0, 0.0).astype(BF16), slab[pl.ds(b * SHARD_ROWS, SHARD_ROWS), :])
        packed[pl.ds(b * PIV_MOST, PIV_MOST), :] = part.astype(BF16)
    for copy in copies:
        copy.wait()


def pick(meta, piv, slab, share):
    depth = slab.shape[1]
    return pl.pallas_call(
        lambda *refs: pick_kernel(share, *refs),
        out_shape=(
            jax.ShapeDtypeStruct((PICKS, depth), BF16),
            jax.ShapeDtypeStruct((2, PICKS, K // 2), BF16),
            jax.ShapeDtypeStruct((SHARD_ROWS, depth), BF16),
        ),
        in_specs=[SMEM, VMEM, VMEM],
        out_specs=(VMEM, VMEM, HBM),
        scratch_shapes=[pltpu.SemaphoreType.DMA((8,))],
        compiler_params=pltpu.CompilerParams(vmem_limit_bytes=22 * MIB),
        cost_estimate=pl.CostEstimate(flops=4 * 10**9, bytes_accessed=14 * MIB, transcendentals=0),
        name="pick_pivot_rows",
    )(meta, piv, slab)


def pivot_kernel(share, meta, place, packed, packed_theirs, gauss, gauss_theirs,
                 u_keep, u_send, l_keep, l_send, code_v, power_v, u_scr, l_scr):
    r, c = meta[0], meta[1]
    x, y = r & 1, (r >> 1) & 1
    rows = dot(packed[...], gauss[...]) + dot(packed_theirs[...], gauss_theirs[...])
    lane = lax.broadcasted_iota(I32, (PICKS, BLK), 1)
    powers = jnp.zeros((PICKS, BLK), F32)
    highs, lows = [], []
    for j in range(NBLK):
        part = rows[:, j * BLK:(j + 1) * BLK]
        most = jnp.max(jnp.abs(part), axis=1, keepdims=True)
        power = jnp.where(most > 0.0, jnp.ceil(jnp.log2(jnp.maximum(most, 1e-30)) + 0.001), 0.0)
        code = jnp.floor(part * jnp.exp2(15.0 - power) + 0.5)
        code = jnp.clip(code, -32767.0, 32767.0)
        high = jnp.floor(code * (1.0 / 256.0))
        highs.append(high.astype(BF16))
        lows.append((code - 256.0 * high).astype(BF16))
        powers = jnp.where(lane == j, power, powers)
    spread = dot(place[c], jnp.concatenate(highs + lows + [powers.astype(BF16)], axis=1), ((0,), (0,)))
    code_v[...] = (spread[:, :K] * 256.0 + spread[:, K:2 * K]).astype(I32).astype(I16)
    power_v[...] = spread[:, 2 * K:]

    columns = lower_layout(share)
    lane = lax.broadcasted_iota(I32, (SUB, BLK), 1)
    lane_l = lax.broadcasted_iota(I32, (share, BLK), 1)
    for quarter in range(4):
        gy, gx = quarter >> 1, quarter & 1
        slot = quarter_slot(gx, gy, x, y, c)
        tail = jnp.zeros((SUB, BLK), F32)
        for n, (i, j) in enumerate(UPPER):
            at = pl.ds(i * (BLK // 2) + quarter * SUB, SUB)
            u_scr[slot, n] = code_v[at, pl.ds(j * BLK, BLK)]
            tail = jnp.where(lane == n, power_v[at, j:j + 1], tail)
        u_scr[slot, len(UPPER)] = tail.astype(I32).astype(I16)
        n = 0
        tail = jnp.zeros((share, BLK), F32)
        for z, count in enumerate(columns):
            at = pl.ds((z * 4 + quarter) * share, share)
            for j in range(count):
                l_scr[slot, n] = code_v[at, pl.ds(j * BLK, BLK)].astype(l_scr.dtype)
                tail = jnp.where(lane_l == z * NBLK + j, power_v[at, j:j + 1], tail)
                n += 1
        l_scr[slot, n] = tail.astype(I32).astype(l_scr.dtype)
    u_keep[...] = u_scr[0:2]
    u_send[...] = u_scr[2:4]
    l_keep[...] = l_scr[0:2]
    l_send[...] = l_scr[2:4]


def pivot_rows(meta, place, packed, packed_theirs, gauss, gauss_theirs, share):
    units = sum(lower_layout(share)) + 1
    u_shape = (len(UPPER) + 1, SUB, BLK)
    l_shape = (units, share, BLK)
    l_type = I16 if share % SUB == 0 else I32
    u_out = jax.ShapeDtypeStruct((2,) + u_shape, I16)
    l_out = jax.ShapeDtypeStruct((2,) + l_shape, l_type)
    return pl.pallas_call(
        lambda *refs: pivot_kernel(share, *refs),
        out_shape=(u_out, u_out, l_out, l_out),
        in_specs=[SMEM] + [VMEM] * 5,
        out_specs=(VMEM,) * 4,
        scratch_shapes=[
            pltpu.VMEM((K // 2, K), I16),
            pltpu.VMEM((K // 2, BLK), F32),
            pltpu.VMEM((4,) + u_shape, I16),
            pltpu.VMEM((4,) + l_shape, l_type),
        ],
        compiler_params=pltpu.CompilerParams(vmem_limit_bytes=24 * MIB),
        cost_estimate=pl.CostEstimate(flops=3 * 10**9, bytes_accessed=8 * MIB, transcendentals=0),
        name="pivot_rows",
    )(meta, place, packed, packed_theirs, gauss, gauss_theirs)


def sketch_kernel(first, meta, slab, theirs, gauss, gauss_theirs, later, out, mark, theirs_v, sems):
    rows = out.shape[0]
    tiles = [pl.ds(t, min(2 * PIECE, rows - t)) for t in range(0, rows, 2 * PIECE)]
    loads = [Copies(theirs.at[pl.ds(first + t.start, t.size)], theirs_v.at[t], sems.at[n]) for n, t in enumerate(tiles)]
    for copy in loads:
        copy.start()
    mark[...] = jnp.zeros_like(mark)
    for n, t in enumerate(tiles):
        mine = pl.ds(pl.multiple_of(meta[1] * theirs.shape[0] + first + t.start, PIECE), t.size)
        total = dot(slab[mine, :], gauss[...])
        loads[n].wait()
        high, low = split(total + dot(theirs_v[t, :], gauss_theirs[...]))
        for s in range(NWIDE):
            cols = slice(s * WIDE, (s + 1) * WIDE)
            out[t, pl.ds(2 * s * WIDE, WIDE)] = high[:, cols]
            out[t, pl.ds((2 * s + 1) * WIDE, WIDE)] = low[:, cols]


def sketch_rows(meta, slab, theirs, gauss, gauss_theirs, first, rows, later):
    depth = theirs.shape[1]
    return pl.pallas_call(
        lambda *refs: sketch_kernel(first, *refs),
        out_shape=(jax.ShapeDtypeStruct((rows, 2 * K), BF16), jax.ShapeDtypeStruct((SUB, BLK), I16)),
        in_specs=[SMEM, VMEM, HBM, VMEM, VMEM, HBM],
        out_specs=(VMEM, VMEM),
        scratch_shapes=[pltpu.VMEM((rows, depth), BF16), pltpu.SemaphoreType.DMA((-(-rows // (2 * PIECE)), 4))],
        compiler_params=pltpu.CompilerParams(vmem_limit_bytes=26 * MIB),
        cost_estimate=pl.CostEstimate(
            flops=4 * rows * depth * K, bytes_accessed=10 * MIB, transcendentals=0),
        name="sketch_rows",
    )(meta, slab, theirs, gauss, gauss_theirs, later)


def store_three(weights, row, cols, value):
    high, low = split(value)
    weights[pl.ds(row, WIDE), cols] = high
    weights[pl.ds(row + WIDE, WIDE), cols] = high
    weights[pl.ds(row + 2 * WIDE, WIDE), cols] = low


def prepare(share, r, c, inverses, pieces, low, own_rows, coupling, weights):
    x, y = r & 1, (r >> 1) & 1
    lane = lax.broadcasted_iota(I32, (SUB, BLK), 1)
    slot = 0
    chunk = min(SUB, share)
    for piece in pieces:
        for k in range(piece.shape[0]):
            gc = c ^ (slot >> 2)
            high, less = (slot >> 1) & 1, slot & 1
            dx, dy = jnp.where(gc == 0, high, less), jnp.where(gc == 0, less, high)
            quarter = (y ^ dy) * 2 + (x ^ dx)
            scales = jnp.exp2(piece[k, len(UPPER)].astype(I32).astype(F32) - 15.0) * (-1.0 / K**0.5)
            for i in range(NBLK - 1):
                starts = []
                for part in range(SUB // chunk):
                    s = i * (BLK // 2) + quarter * SUB + part * chunk
                    owner = lax.div(s, share)
                    starts.append(pl.multiple_of((owner * 2 + gc) * share + (s - owner * share), 8))
                for n, (row_block, j) in enumerate(UPPER):
                    if row_block != i:
                        continue
                    value = piece[k, n].astype(I32).astype(F32) * scales[:, n:n + 1]
                    for part in range(SUB // chunk):
                        coupling[pl.ds(starts[part], chunk), pl.ds(j * BLK, BLK)] = (
                            value[part * chunk:(part + 1) * chunk])
            slot += 1

    own = (r * 2 + c) * share
    up = coupling[pl.ds(pl.multiple_of(own, 8), share), :] * (-(K**0.5))
    tail = low[NBLK].astype(I32)
    place = lax.broadcasted_iota(I32, (share, BLK), 1) - (r >> 2) * NBLK
    diagonal = lax.div(own, BLK)
    for j in range(NBLK):
        power = jnp.sum(jnp.where(place == j, tail, 0), axis=1, keepdims=True).astype(F32)
        value = low[j].astype(I32).astype(F32) * jnp.exp2(power - 15.0)
        cols = pl.ds(j * BLK, BLK)
        own_rows[:, cols] = jnp.where(j > diagonal, up[:, j * BLK:(j + 1) * BLK], value)

    for s in range(NWIDE):
        first, second = inverses[2 * s], inverses[2 * s + 1]
        link = coupling[pl.ds(2 * s * BLK, BLK), pl.ds((2 * s + 1) * BLK, BLK)]
        corner = product(first, product(link, second))
        block = jnp.concatenate([
            jnp.concatenate([first, corner], axis=1),
            jnp.concatenate([jnp.zeros_like(first), second], axis=1)], axis=0)
        cols = pl.ds(s * WIDE, WIDE)
        store_three(weights, 0, cols, block)
        if s > 0:
            turned = product(coupling[pl.ds(0, s * WIDE), cols], block)
            for e in range(s):
                store_three(weights, 3 * (e + 1) * WIDE, cols, turned[e * WIDE:(e + 1) * WIDE])


def solve_kernel(share, parts, meta, *refs):
    sketches, refs = refs[:parts], refs[parts:]
    (inverses, p0, p1, p2, p3, low, out, own_rows,
     coupling, weights, earlier, pair_v, out_v, in_sems, out_sems) = refs
    tile = out_v.shape[1]
    steps = out.shape[0] // tile

    def start_in(step):
        slot = lax.rem(step, 2)
        for h in range(tile // PIECE):
            piece, first = step * (tile // PIECE) + h, 0
            for sketch in sketches:
                count = sketch.shape[0] // PIECE

                @pl.when((piece >= first) & (piece < first + count))
                def _():
                    where = pl.ds(pl.multiple_of((piece - first) * PIECE, PIECE), PIECE)
                    pltpu.make_async_copy(
                        sketch.at[where], pair_v.at[slot, pl.ds(h * PIECE, PIECE)], in_sems.at[slot, h]).start()
                first += count

    def copy_out(step):
        slot = lax.rem(step, 2)
        where = pl.ds(pl.multiple_of(step * tile, tile), tile)
        return pltpu.make_async_copy(out_v.at[slot], out.at[where], out_sems.at[slot])

    start_in(jnp.int32(0))
    start_in(jnp.int32(1))
    prepare(share, meta[0], meta[1], inverses, (p0, p1, p2, p3), low, own_rows, coupling, weights)
    sub = 256

    @pl.loop(0, steps)
    def _(step):
        slot = lax.rem(step, 2)

        @pl.when(step >= 2)
        def _():
            copy_out(step - 2).wait()

        for h in range(tile // PIECE):
            pltpu.make_async_copy(
                sketches[0].at[pl.ds(0, PIECE)], pair_v.at[slot, pl.ds(h * PIECE, PIECE)], in_sems.at[slot, h]).wait()
        for s in range(NWIDE):
            cols = pl.ds(s * WIDE, WIDE)
            for q in range(tile // sub):
                here = pl.ds(q * sub, sub)
                pair = pair_v[slot, here, pl.ds(2 * s * WIDE, 2 * WIDE)]
                high = pair_v[slot, here, pl.ds(2 * s * WIDE, WIDE)]
                acc = dot(pair, weights[pl.ds(0, 2 * WIDE), cols]) + dot(high, weights[pl.ds(2 * WIDE, WIDE), cols])
                if s > 0:
                    depth = 3 * s * WIDE
                    acc = acc + dot(earlier[here, pl.ds(0, depth)], weights[pl.ds(3 * WIDE, depth), cols])
                out_v[slot, here, cols] = acc
                if s < NWIDE - 1:
                    high, low_part = split(acc)
                    to = 3 * s * WIDE
                    earlier[here, pl.ds(to, WIDE)] = high
                    earlier[here, pl.ds(to + WIDE, WIDE)] = low_part
                    earlier[here, pl.ds(to + 2 * WIDE, WIDE)] = high
        copy_out(step).start()

        @pl.when(step + 2 < steps)
        def _():
            start_in(step + 2)

    for step in range(2):
        copy_out(jnp.int32(steps - 2 + step)).wait()


def solve(meta, sketches, inverses, pieces, low, share):
    parts = len(sketches)
    rows = sum(s.shape[0] for s in sketches)
    tile = 512
    return pl.pallas_call(
        lambda *refs: solve_kernel(share, parts, *refs),
        out_shape=(jax.ShapeDtypeStruct((rows, K), F32), jax.ShapeDtypeStruct((share, K), F32)),
        in_specs=[SMEM] + [HBM] * parts + [VMEM] * (2 + len(pieces)),
        out_specs=(HBM, VMEM),
        scratch_shapes=[
            pltpu.VMEM((K, K), F32),
            pltpu.VMEM((3 * K, K), BF16),
            pltpu.VMEM((tile, 3 * (NWIDE - 1) * WIDE), BF16),
            pltpu.VMEM((2, tile, 2 * K), BF16),
            pltpu.VMEM((2, tile, K), F32),
            pltpu.SemaphoreType.DMA((2, tile // PIECE)),
            pltpu.SemaphoreType.DMA((2,)),
        ],
        compiler_params=pltpu.CompilerParams(vmem_limit_bytes=52 * MIB),
        cost_estimate=pl.CostEstimate(flops=8 * 10**9, bytes_accessed=20 * MIB, transcendentals=0),
        name="blocked_solve",
    )(meta, *sketches, inverses, *pieces, low)


def after(value, *others):
    return lax.optimization_barrier((value,) + others)[0]


def on_device(slab, gauss, pivots, block_inverses):
    rows = lax.axis_size("row")
    cols = lax.axis_size("col")
    bits = rows.bit_length() - 1
    tops = bits - 2
    share = K // (rows * cols)
    r, c = lax.axis_index("row"), lax.axis_index("col")
    meta = jnp.stack([r, c]).astype(I32)

    def swap(value, bit_of):
        perm = [(2 * i + k, 2 * (i ^ (1 << bit_of[k])) + k) for i in range(rows) for k in range(2)]
        return lax.ppermute(value, ("row", "col"), perm)

    def swap_cores(value):
        return lax.ppermute(value, "col", [(0, 1), (1, 0)])

    near, far = (0, 1), (1, 0)
    climb = [(2 + s, 2 + (s + 1) % tops) for s in range(tops)]

    gauss_theirs = swap_cores(gauss)
    packed, place, slab_away = pick(meta, pivots.reshape(1, K), slab, share)
    packed_theirs = swap_cores(packed + gauss_theirs[:1] * 0)
    slab_away, mark = lax.optimization_barrier((slab_away, packed_theirs[:SUB, :BLK]))
    slab_theirs = swap_cores(slab_away)
    u_keep, u_send, l_keep, l_send = pivot_rows(
        meta, place, packed, packed_theirs, gauss, gauss_theirs, share)


    rest = slab.shape[0] // cols * 3 // 8
    bounds = (0, slab.shape[0] // cols - rest, slab.shape[0] // cols)

    def sketch_part(part, later):
        first, end = bounds[part:part + 2]
        return sketch_rows(meta, slab, slab_theirs, gauss, gauss_theirs, first, end - first, later)

    size, l_shape = u_keep[0].size // BLK, l_keep.shape[1:]

    def join(upper, lower):
        count = upper.shape[0]
        return jnp.concatenate(
            [upper.reshape(count, -1, BLK), lower.astype(I16).reshape(count, -1, BLK)], axis=1)

    keep, send = join(u_keep, l_keep), join(u_send, l_send)
    sketch, mark = sketch_part(0, mark)
    sketches = [sketch]
    got = swap(send, near) + mark[:1]
    send = keep[1:2] + got[1:2]
    kept = keep[0:1] + got[0:1]
    sketch, mark = sketch_part(1, send)
    sketches.append(sketch)
    kept = kept + (swap(send, far) + mark[:1])
    total = kept[:, :size].reshape(u_keep[:1].shape)
    low = kept[0, size:].reshape(l_shape)
    spread, n = [], 0
    for count in lower_layout(share):
        block = jnp.pad(low[n:n + count], ((0, NBLK - count), (0, 0), (0, 0)))
        spread.append(jnp.concatenate([block, low[-1:]], axis=0))
        n += count
    spread = jnp.stack(spread)
    order = []
    for k in range(1 << tops):
        at = r >> 2
        for s in range(tops):
            if (k >> (tops - 1 - s)) & 1:
                at = at ^ jnp.where(c == 0, 1 << (climb[s][0] - 2), 1 << (climb[s][1] - 2))
        order.append(lax.dynamic_index_in_dim(spread, at, 0, keepdims=False))
    low = jnp.stack(order)
    for s, bit_of in enumerate(climb):
        got = swap(total, bit_of)
        if s == 0:
            low = after(low, got)
        total = total + got
    got = swap(total, far)
    for bit_of in climb:
        half = low.shape[0] // 2
        low_got = swap(low[half:], bit_of)
        low = low[:half] + low_got
    piece1 = got
    pair = jnp.concatenate([total, piece1], axis=0)
    piece2 = after(swap(pair, near), low_got)
    piece3 = swap_cores(jnp.concatenate([pair, piece2], axis=0))
    return solve(meta, sketches, block_inverses, (total, piece1, piece2, piece3), low[0], share)


def solution(mesh):
    return jax.shard_map(
        on_device,
        mesh=mesh,
        in_specs=(P("row", "col"), P("col", None), P(), P()),
        out_specs=(P(("row", "col"), None), P(("row", "col"), None)),
        check_vma=False,
    )
```

```python
import jax
import jax.numpy as jnp
from jax import lax
from jax.experimental import pallas as pl
from jax.experimental.pallas import tpu as pltpu
from jax.sharding import PartitionSpec as P

K = 1024
BLK = 128
NBLK = K // BLK
WIDE = 2 * BLK
NWIDE = K // WIDE
SHARD_ROWS = 2048
PIV_MOST = 128
PICKS = 2 * PIV_MOST
PIECE = 256
SUB = 16
UPPER = [(i, j) for i in range(NBLK) for j in range(i + 1, NBLK)]
F32 = jnp.float32
BF16 = jnp.bfloat16
I16 = jnp.int16
I32 = jnp.int32
MIB = 1 << 20
VMEM = pl.BlockSpec(memory_space=pltpu.VMEM)
SMEM = pl.BlockSpec(memory_space=pltpu.SMEM)
HBM = pl.BlockSpec(memory_space=pltpu.HBM)


def dot(a, b, dims=((1,), (0,))):
    return lax.dot_general(a, b, (dims, ((), ())), preferred_element_type=F32)


def split(a):
    high = a.astype(BF16)
    return high, (a - high.astype(F32)).astype(BF16)


def product(a, b):
    (ah, al), (bh, bl) = split(a), split(b)
    return dot(ah, bh) + (dot(al, bh) + dot(ah, bl))


def quarter_slot(gx, gy, x, y, c):
    dx, dy = gx ^ x, gy ^ y
    return jnp.where(c == 0, dx * 2 + dy, dy * 2 + dx)


class Copies:
    def __init__(self, source, target, sems):
        count = sems.shape[0]
        rows = target.shape[0] // count
        self.parts = [
            pltpu.make_async_copy(source.at[pl.ds(t * rows, rows)], target.at[pl.ds(t * rows, rows)], sems.at[t])
            for t in range(count)
        ]

    def start(self):
        for part in self.parts:
            part.start()

    def wait(self):
        for part in self.parts:
            part.wait()


def lower_layout(share):
    tops = K // (8 * share)
    return [-(-((z + 1) * 8 * share) // BLK) for z in range(tops)]


def by_core(row, share):
    count = row.shape[1] // (2 * share)
    return jnp.concatenate(
        [row[:, (2 * k + core) * share:(2 * k + core + 1) * share] for core in range(2) for k in range(count)], axis=1)


def pick_kernel(share, meta, piv, slab, packed, place, away, sem):
    r, c = meta[0], meta[1]
    part = SHARD_ROWS // 8
    copies = [
        pltpu.make_async_copy(
            slab.at[pl.ds(pl.multiple_of((1 - c) * SHARD_ROWS + t * part, part), part)],
            away.at[pl.ds(t * part, part)], sem.at[t])
        for t in range(8)
    ]
    for copy in copies:
        copy.start()
    half = lax.broadcasted_iota(I32, (8, K), 0)
    local = by_core(piv[...], share) - (r * (2 * SHARD_ROWS) + half * SHARD_ROWS)
    inside = (local >= 0) & (local < SHARD_ROWS) & (half < 2)
    earlier = lax.broadcasted_iota(I32, (K, K), 0) < lax.broadcasted_iota(I32, (K, K), 1)
    rank = dot(jnp.where(inside, 1.0, 0.0).astype(BF16), jnp.where(earlier, 1.0, 0.0).astype(BF16))
    rank = jnp.where(inside, rank, -1.0)
    order = lax.broadcasted_iota(I32, (PIV_MOST, K), 0).astype(F32)
    rows = lax.broadcasted_iota(I32, (PIV_MOST, SHARD_ROWS), 1).astype(F32)
    for b in range(2):
        hit = rank[b:b + 1, :] == order
        one = jnp.where(hit, 1.0, 0.0).astype(BF16)
        for core in range(2):
            place[core, pl.ds(b * PIV_MOST, PIV_MOST), :] = one[:, core * (K // 2):(core + 1) * (K // 2)]
        row = jnp.sum(jnp.where(hit, local[b:b + 1, :].astype(F32), 0.0), axis=1, keepdims=True)
        part = dot(jnp.where(rows == row, 1.0, 0.0).astype(BF16), slab[pl.ds(b * SHARD_ROWS, SHARD_ROWS), :])
        packed[pl.ds(b * PIV_MOST, PIV_MOST), :] = part.astype(BF16)
    for copy in copies:
        copy.wait()


def pick(meta, piv, slab, share):
    depth = slab.shape[1]
    return pl.pallas_call(
        lambda *refs: pick_kernel(share, *refs),
        out_shape=(
            jax.ShapeDtypeStruct((PICKS, depth), BF16),
            jax.ShapeDtypeStruct((2, PICKS, K // 2), BF16),
            jax.ShapeDtypeStruct((SHARD_ROWS, depth), BF16),
        ),
        in_specs=[SMEM, VMEM, VMEM],
        out_specs=(VMEM, VMEM, HBM),
        scratch_shapes=[pltpu.SemaphoreType.DMA((8,))],
        compiler_params=pltpu.CompilerParams(vmem_limit_bytes=22 * MIB),
        cost_estimate=pl.CostEstimate(flops=4 * 10**9, bytes_accessed=14 * MIB, transcendentals=0),
        name="pick_pivot_rows",
    )(meta, piv, slab)


def pivot_kernel(share, meta, place, packed, packed_theirs, gauss, gauss_theirs,
                 u_keep, u_send, l_keep, l_send, code_v, power_v, u_scr, l_scr):
    r, c = meta[0], meta[1]
    x, y = r & 1, (r >> 1) & 1
    rows = dot(packed[...], gauss[...]) + dot(packed_theirs[...], gauss_theirs[...])
    lane = lax.broadcasted_iota(I32, (PICKS, BLK), 1)
    powers = jnp.zeros((PICKS, BLK), F32)
    highs, lows = [], []
    for j in range(NBLK):
        part = rows[:, j * BLK:(j + 1) * BLK]
        most = jnp.max(jnp.abs(part), axis=1, keepdims=True)
        power = jnp.where(most > 0.0, jnp.ceil(jnp.log2(jnp.maximum(most, 1e-30)) + 0.001), 0.0)
        code = jnp.floor(part * jnp.exp2(15.0 - power) + 0.5)
        code = jnp.clip(code, -32767.0, 32767.0)
        high = jnp.floor(code * (1.0 / 256.0))
        highs.append(high.astype(BF16))
        lows.append((code - 256.0 * high).astype(BF16))
        powers = jnp.where(lane == j, power, powers)
    spread = dot(place[c], jnp.concatenate(highs + lows + [powers.astype(BF16)], axis=1), ((0,), (0,)))
    code_v[...] = (spread[:, :K] * 256.0 + spread[:, K:2 * K]).astype(I32).astype(I16)
    power_v[...] = spread[:, 2 * K:]

    columns = lower_layout(share)
    lane = lax.broadcasted_iota(I32, (SUB, BLK), 1)
    lane_l = lax.broadcasted_iota(I32, (share, BLK), 1)
    for quarter in range(4):
        gy, gx = quarter >> 1, quarter & 1
        slot = quarter_slot(gx, gy, x, y, c)
        tail = jnp.zeros((SUB, BLK), F32)
        for n, (i, j) in enumerate(UPPER):
            at = pl.ds(i * (BLK // 2) + quarter * SUB, SUB)
            u_scr[slot, n] = code_v[at, pl.ds(j * BLK, BLK)]
            tail = jnp.where(lane == n, power_v[at, j:j + 1], tail)
        u_scr[slot, len(UPPER)] = tail.astype(I32).astype(I16)
        n = 0
        tail = jnp.zeros((share, BLK), F32)
        for z, count in enumerate(columns):
            at = pl.ds((z * 4 + quarter) * share, share)
            for j in range(count):
                l_scr[slot, n] = code_v[at, pl.ds(j * BLK, BLK)].astype(l_scr.dtype)
                tail = jnp.where(lane_l == z * NBLK + j, power_v[at, j:j + 1], tail)
                n += 1
        l_scr[slot, n] = tail.astype(I32).astype(l_scr.dtype)
    u_keep[...] = u_scr[0:2]
    u_send[...] = u_scr[2:4]
    l_keep[...] = l_scr[0:2]
    l_send[...] = l_scr[2:4]


def pivot_rows(meta, place, packed, packed_theirs, gauss, gauss_theirs, share):
    units = sum(lower_layout(share)) + 1
    u_shape = (len(UPPER) + 1, SUB, BLK)
    l_shape = (units, share, BLK)
    l_type = I16 if share % SUB == 0 else I32
    u_out = jax.ShapeDtypeStruct((2,) + u_shape, I16)
    l_out = jax.ShapeDtypeStruct((2,) + l_shape, l_type)
    return pl.pallas_call(
        lambda *refs: pivot_kernel(share, *refs),
        out_shape=(u_out, u_out, l_out, l_out),
        in_specs=[SMEM] + [VMEM] * 5,
        out_specs=(VMEM,) * 4,
        scratch_shapes=[
            pltpu.VMEM((K // 2, K), I16),
            pltpu.VMEM((K // 2, BLK), F32),
            pltpu.VMEM((4,) + u_shape, I16),
            pltpu.VMEM((4,) + l_shape, l_type),
        ],
        compiler_params=pltpu.CompilerParams(vmem_limit_bytes=24 * MIB),
        cost_estimate=pl.CostEstimate(flops=3 * 10**9, bytes_accessed=8 * MIB, transcendentals=0),
        name="pivot_rows",
    )(meta, place, packed, packed_theirs, gauss, gauss_theirs)


def sketch_kernel(first, meta, slab, theirs, gauss, gauss_theirs, later, out, mark, theirs_v, sems):
    rows = out.shape[0]
    tiles = [pl.ds(t, min(2 * PIECE, rows - t)) for t in range(0, rows, 2 * PIECE)]
    loads = [Copies(theirs.at[pl.ds(first + t.start, t.size)], theirs_v.at[t], sems.at[n]) for n, t in enumerate(tiles)]
    for copy in loads:
        copy.start()
    mark[...] = jnp.zeros_like(mark)
    for n, t in enumerate(tiles):
        mine = pl.ds(pl.multiple_of(meta[1] * theirs.shape[0] + first + t.start, PIECE), t.size)
        total = dot(slab[mine, :], gauss[...])
        loads[n].wait()
        high, low = split(total + dot(theirs_v[t, :], gauss_theirs[...]))
        for s in range(NWIDE):
            cols = slice(s * WIDE, (s + 1) * WIDE)
            out[t, pl.ds(2 * s * WIDE, WIDE)] = high[:, cols]
            out[t, pl.ds((2 * s + 1) * WIDE, WIDE)] = low[:, cols]


def sketch_rows(meta, slab, theirs, gauss, gauss_theirs, first, rows, later):
    depth = theirs.shape[1]
    return pl.pallas_call(
        lambda *refs: sketch_kernel(first, *refs),
        out_shape=(jax.ShapeDtypeStruct((rows, 2 * K), BF16), jax.ShapeDtypeStruct((SUB, BLK), I16)),
        in_specs=[SMEM, VMEM, HBM, VMEM, VMEM, HBM],
        out_specs=(VMEM, VMEM),
        scratch_shapes=[pltpu.VMEM((rows, depth), BF16), pltpu.SemaphoreType.DMA((-(-rows // (2 * PIECE)), 4))],
        compiler_params=pltpu.CompilerParams(vmem_limit_bytes=26 * MIB),
        cost_estimate=pl.CostEstimate(
            flops=4 * rows * depth * K, bytes_accessed=10 * MIB, transcendentals=0),
        name="sketch_rows",
    )(meta, slab, theirs, gauss, gauss_theirs, later)


def store_three(weights, row, cols, value):
    high, low = split(value)
    weights[pl.ds(row, WIDE), cols] = high
    weights[pl.ds(row + WIDE, WIDE), cols] = high
    weights[pl.ds(row + 2 * WIDE, WIDE), cols] = low


def prepare(share, r, c, inverses, pieces, low, own_rows, coupling, weights):
    x, y = r & 1, (r >> 1) & 1
    lane = lax.broadcasted_iota(I32, (SUB, BLK), 1)
    slot = 0
    chunk = min(SUB, share)
    for piece in pieces:
        for k in range(piece.shape[0]):
            gc = c ^ (slot >> 2)
            high, less = (slot >> 1) & 1, slot & 1
            dx, dy = jnp.where(gc == 0, high, less), jnp.where(gc == 0, less, high)
            quarter = (y ^ dy) * 2 + (x ^ dx)
            scales = jnp.exp2(piece[k, len(UPPER)].astype(I32).astype(F32) - 15.0) * (-1.0 / K**0.5)
            for i in range(NBLK - 1):
                starts = []
                for part in range(SUB // chunk):
                    s = i * (BLK // 2) + quarter * SUB + part * chunk
                    owner = lax.div(s, share)
                    starts.append(pl.multiple_of((owner * 2 + gc) * share + (s - owner * share), 8))
                for n, (row_block, j) in enumerate(UPPER):
                    if row_block != i:
                        continue
                    value = piece[k, n].astype(I32).astype(F32) * scales[:, n:n + 1]
                    for part in range(SUB // chunk):
                        coupling[pl.ds(starts[part], chunk), pl.ds(j * BLK, BLK)] = (
                            value[part * chunk:(part + 1) * chunk])
            slot += 1

    own = (r * 2 + c) * share
    up = coupling[pl.ds(pl.multiple_of(own, 8), share), :] * (-(K**0.5))
    tail = low[NBLK].astype(I32)
    place = lax.broadcasted_iota(I32, (share, BLK), 1) - (r >> 2) * NBLK
    diagonal = lax.div(own, BLK)
    for j in range(NBLK):
        power = jnp.sum(jnp.where(place == j, tail, 0), axis=1, keepdims=True).astype(F32)
        value = low[j].astype(I32).astype(F32) * jnp.exp2(power - 15.0)
        cols = pl.ds(j * BLK, BLK)
        own_rows[:, cols] = jnp.where(j > diagonal, up[:, j * BLK:(j + 1) * BLK], value)

    for s in range(NWIDE):
        first, second = inverses[2 * s], inverses[2 * s + 1]
        link = coupling[pl.ds(2 * s * BLK, BLK), pl.ds((2 * s + 1) * BLK, BLK)]
        corner = product(first, product(link, second))
        block = jnp.concatenate([
            jnp.concatenate([first, corner], axis=1),
            jnp.concatenate([jnp.zeros_like(first), second], axis=1)], axis=0)
        cols = pl.ds(s * WIDE, WIDE)
        store_three(weights, 0, cols, block)
        if s > 0:
            turned = product(coupling[pl.ds(0, s * WIDE), cols], block)
            for e in range(s):
                store_three(weights, 3 * (e + 1) * WIDE, cols, turned[e * WIDE:(e + 1) * WIDE])


def solve_kernel(share, parts, meta, *refs):
    sketches, refs = refs[:parts], refs[parts:]
    (inverses, p0, p1, p2, p3, p4, low, out, own_rows,
     coupling, weights, earlier, pair_v, out_v, in_sems, out_sems) = refs
    tile = out_v.shape[1]
    steps = out.shape[0] // tile

    def start_in(step):
        slot = lax.rem(step, 2)
        for h in range(tile // PIECE):
            piece, first = step * (tile // PIECE) + h, 0
            for sketch in sketches:
                count = sketch.shape[0] // PIECE

                @pl.when((piece >= first) & (piece < first + count))
                def _():
                    where = pl.ds(pl.multiple_of((piece - first) * PIECE, PIECE), PIECE)
                    pltpu.make_async_copy(
                        sketch.at[where], pair_v.at[slot, pl.ds(h * PIECE, PIECE)], in_sems.at[slot, h]).start()
                first += count

    def copy_out(step):
        slot = lax.rem(step, 2)
        where = pl.ds(pl.multiple_of(step * tile, tile), tile)
        return pltpu.make_async_copy(out_v.at[slot], out.at[where], out_sems.at[slot])

    start_in(jnp.int32(0))
    start_in(jnp.int32(1))
    prepare(share, meta[0], meta[1], inverses, (p0, p1, p2, p3, p4), low, own_rows, coupling, weights)
    sub = 256

    @pl.loop(0, steps)
    def _(step):
        slot = lax.rem(step, 2)

        @pl.when(step >= 2)
        def _():
            copy_out(step - 2).wait()

        for h in range(tile // PIECE):
            pltpu.make_async_copy(
                sketches[0].at[pl.ds(0, PIECE)], pair_v.at[slot, pl.ds(h * PIECE, PIECE)], in_sems.at[slot, h]).wait()
        for s in range(NWIDE):
            cols = pl.ds(s * WIDE, WIDE)
            for q in range(tile // sub):
                here = pl.ds(q * sub, sub)
                pair = pair_v[slot, here, pl.ds(2 * s * WIDE, 2 * WIDE)]
                high = pair_v[slot, here, pl.ds(2 * s * WIDE, WIDE)]
                acc = dot(pair, weights[pl.ds(0, 2 * WIDE), cols]) + dot(high, weights[pl.ds(2 * WIDE, WIDE), cols])
                if s > 0:
                    depth = 3 * s * WIDE
                    acc = acc + dot(earlier[here, pl.ds(0, depth)], weights[pl.ds(3 * WIDE, depth), cols])
                out_v[slot, here, cols] = acc
                if s < NWIDE - 1:
                    high, low_part = split(acc)
                    to = 3 * s * WIDE
                    earlier[here, pl.ds(to, WIDE)] = high
                    earlier[here, pl.ds(to + WIDE, WIDE)] = low_part
                    earlier[here, pl.ds(to + 2 * WIDE, WIDE)] = high
        copy_out(step).start()

        @pl.when(step + 2 < steps)
        def _():
            start_in(step + 2)

    for step in range(2):
        copy_out(jnp.int32(steps - 2 + step)).wait()


def solve(meta, sketches, inverses, pieces, low, share):
    parts = len(sketches)
    rows = sum(s.shape[0] for s in sketches)
    tile = 512
    return pl.pallas_call(
        lambda *refs: solve_kernel(share, parts, *refs),
        out_shape=(jax.ShapeDtypeStruct((rows, K), F32), jax.ShapeDtypeStruct((share, K), F32)),
        in_specs=[SMEM] + [HBM] * parts + [VMEM] * (2 + len(pieces)),
        out_specs=(HBM, VMEM),
        scratch_shapes=[
            pltpu.VMEM((K, K), F32),
            pltpu.VMEM((3 * K, K), BF16),
            pltpu.VMEM((tile, 3 * (NWIDE - 1) * WIDE), BF16),
            pltpu.VMEM((2, tile, 2 * K), BF16),
            pltpu.VMEM((2, tile, K), F32),
            pltpu.SemaphoreType.DMA((2, tile // PIECE)),
            pltpu.SemaphoreType.DMA((2,)),
        ],
        compiler_params=pltpu.CompilerParams(vmem_limit_bytes=52 * MIB),
        cost_estimate=pl.CostEstimate(flops=8 * 10**9, bytes_accessed=20 * MIB, transcendentals=0),
        name="blocked_solve",
    )(meta, *sketches, inverses, *pieces, low)


def after(value, *others):
    return lax.optimization_barrier((value,) + others)[0]


def on_device(slab, gauss, pivots, block_inverses):
    rows = lax.axis_size("row")
    cols = lax.axis_size("col")
    bits = rows.bit_length() - 1
    tops = bits - 2
    share = K // (rows * cols)
    r, c = lax.axis_index("row"), lax.axis_index("col")
    meta = jnp.stack([r, c]).astype(I32)

    def swap(value, bit_of):
        perm = [(2 * i + k, 2 * (i ^ (1 << bit_of[k])) + k) for i in range(rows) for k in range(2)]
        return lax.ppermute(value, ("row", "col"), perm)

    def swap_cores(value):
        return lax.ppermute(value, "col", [(0, 1), (1, 0)])

    near, far = (0, 1), (1, 0)
    climb = [(2 + s, 2 + (s + 1) % tops) for s in range(tops)]

    gauss_theirs = swap_cores(gauss)
    packed, place, slab_away = pick(meta, pivots.reshape(1, K), slab, share)
    packed_theirs = swap_cores(packed + gauss_theirs[:1] * 0)
    slab_away, mark = lax.optimization_barrier((slab_away, packed_theirs[:SUB, :BLK]))
    slab_theirs = swap_cores(slab_away)
    u_keep, u_send, l_keep, l_send = pivot_rows(
        meta, place, packed, packed_theirs, gauss, gauss_theirs, share)


    rest = slab.shape[0] // cols * 3 // 8
    bounds = (0, slab.shape[0] // cols - rest, slab.shape[0] // cols)

    def sketch_part(part, later):
        first, end = bounds[part:part + 2]
        return sketch_rows(meta, slab, slab_theirs, gauss, gauss_theirs, first, end - first, later)

    size, l_shape = u_keep[0].size // BLK, l_keep.shape[1:]

    def join(upper, lower):
        count = upper.shape[0]
        return jnp.concatenate(
            [upper.reshape(count, -1, BLK), lower.astype(I16).reshape(count, -1, BLK)], axis=1)

    keep, send = join(u_keep, l_keep), join(u_send, l_send)
    sketch, mark = sketch_part(0, mark)
    sketches = [sketch]
    got = swap(send, near) + mark[:1]
    send = keep[1:2] + got[1:2]
    kept = keep[0:1] + got[0:1]
    sketch, mark = sketch_part(1, send)
    sketches.append(sketch)
    kept = kept + (swap(send, far) + mark[:1])
    total = kept[:, :size].reshape(u_keep[:1].shape)
    low = kept[0, size:].reshape(l_shape)
    spread, n = [], 0
    for count in lower_layout(share):
        block = jnp.pad(low[n:n + count], ((0, NBLK - count), (0, 0), (0, 0)))
        spread.append(jnp.concatenate([block, low[-1:]], axis=0))
        n += count
    spread = jnp.stack(spread)
    order = []
    for k in range(1 << tops):
        at = r >> 2
        for s in range(tops):
            if (k >> (tops - 1 - s)) & 1:
                at = at ^ jnp.where(c == 0, 1 << (climb[s][0] - 2), 1 << (climb[s][1] - 2))
        order.append(lax.dynamic_index_in_dim(spread, at, 0, keepdims=False))
    low = jnp.stack(order)
    for s, bit_of in enumerate(climb):
        got = swap(total, bit_of)
        if s == 0:
            low = after(low, got)
        total = total + got
    got = swap(total, far)
    for bit_of in climb:
        half = low.shape[0] // 2
        low_got = swap(low[half:], bit_of)
        low = low[:half] + low_got
    piece1 = got
    pair = jnp.concatenate([total, piece1], axis=0)
    piece2 = after(swap(pair, near), low_got)
    piece3, piece4 = swap_cores(pair), swap_cores(piece2)
    return solve(meta, sketches, block_inverses, (total, piece1, piece2, piece3, piece4), low[0], share)


def solution(mesh):
    return jax.shard_map(
        on_device,
        mesh=mesh,
        in_specs=(P("row", "col"), P("col", None), P(), P()),
        out_specs=(P(("row", "col"), None), P(("row", "col"), None)),
        check_vma=False,
    )
```
